512 devices in a mesh: grp: 32 (over y, x), row: 16 (over z, core).
Axes of the slice: x: 4, y: 8, z: 8, core: 2. Of those that a mesh axis runs over, the one named last changes fastest.
Arguments:
- activations: bfloat16 [262144, 4096], P(('grp', 'row')), may hold values from -2200 to 2200
- probe_matrix: bfloat16 [128, 4096], P(None, 'row'), may hold values from -0.09375 to 0.09375
Outputs:
- first_projected: float32 [128, 4096], P(None, ('grp', 'row'))
- projected: float32 [128, 4096], P(None, 'row')
The draws below stay inside these ranges and needn't reach their ends.
All inputs are finite; a program needn't handle non-finite values.
Results may differ from the reference program's by a relative error of at most 0.0032.
Values may be sent and summed in bfloat16 or wider, within the bound.
A program may use at most 64 MiB of HBM per device.

```python
import math
import jax
import jax.numpy as jnp
from jax import lax

D = 4096
K = 128
TOK_DEV = 512
TOKENS = 262144
N_GRP = 32


def draw_activations(key, part):
    key = jax.random.fold_in(key, 17)
    subkeys = jax.random.split(key, 5)
    col_scale = jnp.exp(jax.random.uniform(subkeys[1], (D,), jnp.float32, math.log(0.3), math.log(3.0)))
    position = jnp.arange(TOKENS, dtype=jnp.float32) / max(TOKENS - 1, 1)
    block_count = TOKENS // TOK_DEV
    col_width = D // block_count
    pairing = jax.random.permutation(subkeys[4], block_count)
    token_block = jnp.arange(TOKENS, dtype=jnp.int32) // TOK_DEV
    col_block = jnp.arange(D, dtype=jnp.int32) // col_width
    paired = pairing[token_block][:, None] == col_block[None, :]
    heavy = jnp.where(paired, 16.0, 1.0).astype(jnp.float32)
    row_scale = jnp.exp(jax.random.uniform(subkeys[2], (TOKENS,), jnp.float32, math.log(0.5), math.log(5.0))) * (0.5 + position)
    entries = jax.random.truncated_normal(subkeys[0], -6.0, 6.0, (TOKENS, D), jnp.float32)
    values = entries * col_scale[None, :] * row_scale[:, None] * heavy
    return values.astype(jnp.bfloat16)


def block_levels(own_key, dims, cuts, least, top_value):
    factor_of = 1.0
    for axis_at, blocks in cuts:
        steps = jax.random.uniform(jax.random.fold_in(jax.random.fold_in(own_key, 6), axis_at), (blocks,), jnp.float32, least / len(cuts), top_value / len(cuts))
        factor_of = factor_of * jnp.repeat(jnp.exp(steps), dims[axis_at] // blocks).reshape((-1,) + (1,) * (len(dims) - 1 - axis_at))
    return factor_of


def bell_draw(rng, extent, deviation, bound, shards=(), kind=jnp.bfloat16):
    loudness = block_levels(rng, extent, shards, -0.22, 0.18) if shards else 1.0
    values = jax.random.normal(rng, extent, jnp.float32) * deviation * loudness
    return jnp.minimum(jnp.maximum(values, -bound), bound).astype(kind)


def setup_inputs(seed: int = 0) -> dict:
    arg_keys = jax.random.split(jax.random.key(seed), 3)
    return {
        "activations": draw_activations(jax.random.fold_in(arg_keys[2], 71), 0),
        "probe_matrix": bell_draw(arg_keys[1], (K, D), D ** -0.5, 0.09375, ((1, 16),)),
    }


def solve_lower(gram_term, cross_term):
    factor = jnp.linalg.cholesky(gram_term)
    return jax.scipy.linalg.solve_triangular(factor, cross_term, lower=True)

def reference(activations, probe_matrix):
    group_count = N_GRP
    sketch_cols = probe_matrix.shape[0]
    width_all = activations.shape[1]
    blocks = activations.reshape(group_count, activations.shape[0] // group_count, width_all)

    def first_sketch(act_block):
        return lax.dot_general(probe_matrix.astype(jnp.float32), act_block.astype(jnp.float32), (((1,), (1,)), ((), ())), preferred_element_type=jnp.float32).astype(jnp.bfloat16)

    def moments(running, inputs):
        sketch_block, act_block = inputs
        gram_term = running[0] + lax.dot_general(sketch_block.astype(jnp.float32), sketch_block.astype(jnp.float32), (((1,), (1,)), ((), ())), preferred_element_type=jnp.float32)
        cross_term = running[1] + jnp.dot(sketch_block.astype(jnp.float32), act_block.astype(jnp.float32), preferred_element_type=jnp.float32)
        return ((gram_term, cross_term), None)
    initial = (jnp.zeros((sketch_cols, sketch_cols), jnp.float32), jnp.zeros((sketch_cols, width_all), jnp.float32))
    sketch = lax.map(first_sketch, blocks)
    (gram_one, cross_one), _ = lax.scan(moments, initial, (sketch, blocks))
    first_projected = solve_lower(gram_one, cross_one)
    back_proj = first_projected.astype(jnp.bfloat16)

    def second_sketch(act_block):
        return lax.dot_general(back_proj.astype(jnp.float32), act_block.astype(jnp.float32), (((1,), (1,)), ((), ())), preferred_element_type=jnp.float32).astype(jnp.bfloat16)
    sketch_two = lax.map(second_sketch, blocks)
    (gram_two, cross_two), _ = lax.scan(moments, initial, (sketch_two, blocks))
    return (first_projected, solve_lower(gram_two, cross_two))
```

```python
import jax
import jax.numpy as jnp
from jax import lax
from jax.experimental import pallas as pl
from jax.experimental.pallas import tpu as pltpu
from jax.sharding import PartitionSpec as P

MESH = pl.DeviceIdType.MESH
NX, NY, NZ = 4, 8, 8
ROW = 2 * NZ
K = 128
TOK = 512
D = 4096
F32, BF16 = jnp.float32, jnp.bfloat16
NT = (((1,), (1,)), ((), ()))


def each(low, high, body):
    def step(i, carry):
        body(i)
        return carry

    lax.fori_loop(low, high, step, 0)


def kernel(
    act_hbm, probe_hbm, out_first, out_second,
    act, p_own, p_rel, q_own, q_rel, acc, acc_t, sk,
    g_loc, g_r1, g_s1, g_r2, g_s2, g_r3, g_full, elim_g, elim_x, linv,
    sib_out, sib_in, part, s1, r1a, r1b, t0, t1, r2, u, r3,
    bt, first, second,
    in_sem, probe_sem, gram_sem, cross_sem, gather_sem,
):
    grp, row = lax.axis_index("grp"), lax.axis_index("row")
    y, x = lax.div(grp, NX), lax.rem(grp, NX)
    z, c = lax.div(row, 2), lax.rem(row, 2)

    def z_dev(d):
        return (grp, lax.rem(z + d, NZ) * 2 + c)

    def y_dev(d):
        return (lax.rem(y + d, NY) * NX + x, row)

    def x_dev(d):
        return (y * NX + lax.rem(x + d, NX), row)

    def r_dev(d):
        return (grp, lax.rem(row + d, ROW))

    sib = (grp, row + 1 - 2 * c)

    def send(src, dst, sems, dev):
        pltpu.make_async_remote_copy(
            src_ref=src, dst_ref=dst, send_sem=sems.at[0], recv_sem=sems.at[1],
            device_id=dev, device_id_type=MESH,
        ).start()

    sent = []

    def arrived(ref, sems):
        pltpu.make_async_copy(ref, ref, sems.at[1]).wait()
        sent.append((ref, sems))

    load_act = pltpu.make_async_copy(act_hbm, act, in_sem.at[0])
    load_probe = pltpu.make_async_copy(probe_hbm, p_own, in_sem.at[1])
    load_probe.start()
    load_act.start()

    barrier = pltpu.get_barrier_semaphore()

    def greet(dev):
        pl.semaphore_signal(barrier, inc=1, device_id=dev, device_id_type=MESH)

    each(1, ROW, lambda d: greet(r_dev(d)))
    each(1, NY, lambda d: greet(y_dev(d)))
    each(1, NX, lambda d: greet(x_dev(d)))
    load_probe.wait()
    pl.semaphore_wait(barrier, ROW - 1 + NY - 1 + NX - 1)

    rows_y = pl.ds(pl.multiple_of(lax.rem(y, 4) * 32, 32), 32)
    rows_x = pl.ds(pl.multiple_of(x * 32, 32), 32)
    low, high = pl.ds(0, 128), pl.ds(128, 128)

    def probe_z(d):
        send(p_own.at[rows_y, low], p_rel.at[7 - d, rows_y, low], probe_sem.at[0], z_dev(d))
        send(p_own.at[rows_x, high], p_rel.at[7 - d, rows_x, high], probe_sem.at[1], z_dev(d))

    each(1, NZ, probe_z)
    send(p_own, q_own, probe_sem.at[2], sib)

    def columns(at, width):
        return pl.ds(pl.multiple_of(at, width), width)

    def probe_dot(block, z_at, c_at):
        return lax.dot_general(
            block, act[:, columns((z_at * 2 + c_at) * 256, 256)], NT, preferred_element_type=F32
        )

    arrived(p_rel.at[:, pl.ds(0, 32), low], probe_sem.at[0])
    for d in (1, 7, 2 + 4 * c):
        send(p_rel.at[:, rows_y, low], p_rel.at[:, rows_y, low], probe_sem.at[3], y_dev(d))
    arrived(p_rel.at[:, pl.ds(0, 32), high], probe_sem.at[1])
    for d in (1, 2, 3):
        send(p_rel.at[:, rows_x, high], p_rel.at[:, rows_x, high], probe_sem.at[4], x_dev(d))
    load_act.wait()
    acc[...] = probe_dot(p_own[...], z, c)
    arrived(q_own, probe_sem.at[2])
    acc[...] += probe_dot(q_own[...], z, 1 - c)
    arrived(p_rel.at[:, pl.ds(0, 96), high], probe_sem.at[4])
    send(p_rel.at[:, :, high], q_rel.at[:, :, high], probe_sem.at[5], sib)
    arrived(p_rel.at[:, pl.ds(0, 96), low], probe_sem.at[3])
    send(p_rel.at[:, :, low], q_rel.at[:, :, low], probe_sem.at[6], sib)

    def add_own(d):
        acc[...] += probe_dot(p_rel[d], lax.rem(z + d + 1, NZ), c)

    def add_sib(d):
        acc[...] += probe_dot(q_rel[d], lax.rem(z + d + 1, NZ), 1 - c)

    each(0, NZ - 1, add_own)
    arrived(q_rel.at[:, :, high], probe_sem.at[5])
    arrived(q_rel.at[:, :, low], probe_sem.at[6])
    each(0, NZ - 1, add_sib)
    sk[...] = acc[...].astype(BF16)

    def eliminate(count, rows, start):
        def step(i, carry):
            left, right = elim_g[0:rows, :], elim_x[0:rows, :]
            cols = [jnp.broadcast_to(left[:, j : j + 1], (rows, K)) for j in range(8)]
            g_rows = [left[j : j + 1, :] for j in range(8)]
            x_rows = [right[j : j + 1, :] for j in range(8)]
            for k in range(8):
                scale = lax.rsqrt(cols[k][k : k + 1, :])
                cols[k] = cols[k] * scale
                g_rows[k] = g_rows[k] * scale
                x_rows[k] = x_rows[k] * scale
                for j in range(k + 1, 8):
                    factor = cols[k][j : j + 1, :]
                    cols[j] = cols[j] - cols[k] * factor
                    g_rows[j] = g_rows[j] - g_rows[k] * factor
                    x_rows[j] = x_rows[j] - x_rows[k] * factor
            linv[pl.ds(pl.multiple_of((start + i) * 8, 8), 8), :] = jnp.concatenate(x_rows, axis=0)
            below = [col[8:, :] for col in cols]
            left, right = left[8:, :], right[8:, :]
            for k in range(8):
                left = left - below[k] * g_rows[k]
                right = right - below[k] * x_rows[k]
            elim_g[0 : rows - 8, :] = pltpu.roll(left, K - 8, 1)
            elim_x[0 : rows - 8, :] = right
            return carry

        lax.fori_loop(0, count, step, 0)

    def solve_round(rd, a_at, b_at, a_dev, b_dev):
        gram = gram_sem.at[rd]
        cross = cross_sem.at[rd]
        sketch = sk[...]
        g_loc[rd] = lax.dot_general(sketch, sketch, NT, preferred_element_type=F32).reshape(ROW, 8, K)
        each(1, ROW, lambda d: send(
            g_loc.at[rd, lax.rem(row + d, ROW)], g_r1.at[rd, d - 1], gram.at[0], r_dev(d)))

        def for_sibling(a):
            term = jnp.dot(
                sk[...], act[:, columns(a * 512 + (1 - c) * 256, 256)], preferred_element_type=F32
            )
            sib_out[rd, a] = term.T.astype(BF16)
            send(sib_out.at[rd, a], sib_in.at[rd, a], cross.at[0], sib)

        def for_self(a):
            term = jnp.dot(
                sk[...], act[:, columns(a * 512 + c * 256, 256)], preferred_element_type=F32
            )
            part[a] = term.T.reshape(2, 8, 16, K)

        each(0, 8, for_sibling)
        arrived(g_r1.at[rd], gram.at[0])
        total = g_loc[rd, row]
        for d in range(ROW - 1):
            total = total + g_r1[rd, d]
        g_s1[rd] = total
        each(1, NY, lambda d: send(g_s1.at[rd], g_r2.at[rd, d - 1], gram.at[1], y_dev(d)))
        each(0, 4, for_self)
        arrived(g_r2.at[rd], gram.at[1])
        for d in range(NY - 1):
            total = total + g_r2[rd, d]
        g_s2[rd] = total
        each(1, NX, lambda d: send(g_s2.at[rd], g_r3.at[rd, d - 1], gram.at[2], x_dev(d)))
        each(4, 8, for_self)
        arrived(g_r3.at[rd], gram.at[2])
        for d in range(NX - 1):
            total = total + g_r3[rd, d]
        g_full[rd, row] = total
        each(1, ROW, lambda d: send(g_full.at[rd, row], g_full.at[rd, row], gram.at[3], r_dev(d)))

        arrived(sib_in.at[rd], cross.at[0])

        def combine(a):
            both = part[a] + sib_in[rd, a].astype(F32).reshape(2, 8, 16, K)
            part[a] = both
            s1[rd, a] = both.astype(BF16)

        each(0, 8, combine)
        each(1, 8, lambda d: send(
            s1.at[rd, lax.rem(a_at + d, 8), 0], r1a.at[rd, d - 1], cross.at[1], a_dev(d)))
        each(1, 8, lambda d: send(
            s1.at[rd, :, 1, lax.rem(b_at + d, 8)], r1b.at[rd, d - 1], cross.at[2], b_dev(d)))

        arrived(g_full.at[rd, pl.ds(0, ROW - 1)], gram.at[3])
        elim_g[...] = g_full[rd].reshape(K, K)
        elim_x[...] = (
            lax.broadcasted_iota(jnp.int32, (K, K), 0) == lax.broadcasted_iota(jnp.int32, (K, K), 1)
        ).astype(F32)
        eliminate(4, 128, 0)
        eliminate(4, 96, 4)

        arrived(r1a.at[rd], cross.at[1])
        total_0 = part[a_at, 0]
        for d in range(7):
            total_0 = total_0 + r1a[rd, d].astype(F32)
        t0[rd] = total_0
        each(1, 8, lambda d: send(
            t0.at[rd, lax.rem(b_at + d, 8)], r2.at[rd, 0, d - 1], cross.at[3], b_dev(d)))
        arrived(r1b.at[rd], cross.at[2])
        total_1 = part[:, 1, b_at]
        for d in range(7):
            total_1 = total_1 + r1b[rd, d].astype(F32)
        t1[rd] = total_1
        each(1, 8, lambda d: send(
            t1.at[rd, lax.rem(a_at + d, 8)], r2.at[rd, 1, d - 1], cross.at[4], a_dev(d)))
        eliminate(4, 64, 8)
        arrived(r2.at[rd, 0], cross.at[3])
        arrived(r2.at[rd, 1], cross.at[4])
        sum_0, sum_1 = t0[rd, b_at], t1[rd, a_at]
        for d in range(7):
            sum_0 = sum_0 + r2[rd, 0, d]
            sum_1 = sum_1 + r2[rd, 1, d]
        u[rd, 0] = sum_0
        u[rd, 1] = sum_1
        each(1, NX, lambda d: send(u.at[rd], r3.at[rd, d - 1], cross.at[5], x_dev(d)))
        eliminate(4, 32, 12)
        arrived(r3.at[rd], cross.at[5])
        whole = u[rd]
        for d in range(NX - 1):
            whole = whole + r3[rd, d]
        solved = lax.dot_general(
            whole.reshape(32, K), linv[...], NT, precision=lax.Precision.HIGHEST,
            preferred_element_type=F32,
        )
        return solved.reshape(2, 16, K)

    solved = solve_round(0, y, z, y_dev, z_dev)
    first[c] = solved
    for h in range(2):
        bt[y, 2 * c + h, z] = solved[h].astype(BF16)
    each(1, NZ, lambda d: send(bt.at[y, 2 * c, z], bt.at[y, 2 * c, z], gather_sem.at[0], z_dev(d)))
    each(1, NY, lambda d: send(bt.at[y, 2 * c + 1, z], bt.at[y, 2 * c + 1, z], gather_sem.at[1], y_dev(d)))
    arrived(bt.at[0, 0, pl.ds(0, 7)], gather_sem.at[0])
    each(1, NY, lambda d: send(bt.at[y, 2 * c], bt.at[y, 2 * c], gather_sem.at[2], y_dev(d)))
    arrived(bt.at[0, 0, pl.ds(0, 7)], gather_sem.at[1])
    each(1, NZ, lambda d: send(bt.at[:, 2 * c + 1, z], bt.at[:, 2 * c + 1, z], gather_sem.at[3], z_dev(d)))
    send(first.at[c], first.at[c], gather_sem.at[6], sib)
    arrived(bt.at[pl.ds(0, 7), 0], gather_sem.at[2])
    send(bt.at[:, 2 * c], bt.at[:, 2 * c], gather_sem.at[4], sib)
    arrived(bt.at[pl.ds(0, 7), 0], gather_sem.at[3])
    send(bt.at[:, 2 * c + 1], bt.at[:, 2 * c + 1], gather_sem.at[5], sib)

    def back_dot(a, c_at):
        return jnp.dot(
            act[:, columns(a * 512 + c_at * 256, 256)],
            bt[a, pl.ds(2 * c_at, 2)].reshape(256, K),
            preferred_element_type=F32,
        )

    acc_t[...] = back_dot(0, c)

    def add_back(c_at):
        def add(a):
            acc_t[...] += back_dot(a, c_at)

        return add

    each(1, 8, add_back(c))
    arrived(bt.at[:, 0], gather_sem.at[4])
    arrived(bt.at[:, 0], gather_sem.at[5])
    each(0, 8, add_back(1 - c))
    sk[...] = acc_t[...].T.astype(BF16)

    solved = solve_round(1, z, y, z_dev, y_dev)
    second[:, y] = solved
    each(1, NY, lambda d: send(second.at[:, y], second.at[:, y], gather_sem.at[7], y_dev(d)))
    arrived(first.at[0], gather_sem.at[6])
    out_first[...] = first[lax.div(x, 2), lax.rem(x, 2), pl.ds(pl.multiple_of(8 * c, 8), 8), :]
    arrived(second.at[:, pl.ds(0, 7)], gather_sem.at[7])
    out_second[...] = second[...].reshape(256, K)
    for ref, sems in sent:
        pltpu.make_async_copy(ref, ref, sems.at[0]).wait()


def on_device(activations, probe_matrix):
    vmem = pltpu.VMEM
    first_t, second_t = pl.pallas_call(
        kernel,
        out_shape=(
            jax.ShapeDtypeStruct((8, K), F32),
            jax.ShapeDtypeStruct((256, K), F32),
        ),
        in_specs=[pl.BlockSpec(memory_space=pl.ANY)] * 2,
        out_specs=(
            pl.BlockSpec(memory_space=pltpu.VMEM),
            pl.BlockSpec(memory_space=pltpu.VMEM),
        ),
        scratch_shapes=[
            vmem((TOK, D), BF16),
            vmem((K, 256), BF16),
            vmem((7, K, 256), BF16),
            vmem((K, 256), BF16),
            vmem((7, K, 256), BF16),
            vmem((K, TOK), F32),
            vmem((TOK, K), F32),
            vmem((K, TOK), BF16),
            vmem((2, ROW, 8, K), F32),
            vmem((2, ROW - 1, 8, K), F32),
            vmem((2, 8, K), F32),
            vmem((2, NY - 1, 8, K), F32),
            vmem((2, 8, K), F32),
            vmem((2, NX - 1, 8, K), F32),
            vmem((2, ROW, 8, K), F32),
            vmem((K, K), F32),
            vmem((K, K), F32),
            vmem((K, K), F32),
            vmem((2, 8, 256, K), BF16),
            vmem((2, 8, 256, K), BF16),
            vmem((8, 2, 8, 16, K), F32),
            vmem((2, 8, 2, 8, 16, K), BF16),
            vmem((2, 7, 8, 16, K), BF16),
            vmem((2, 7, 8, 16, K), BF16),
            vmem((2, 8, 16, K), F32),
            vmem((2, 8, 16, K), F32),
            vmem((2, 2, 7, 16, K), F32),
            vmem((2, 2, 16, K), F32),
            vmem((2, NX - 1, 2, 16, K), F32),
            vmem((8, 4, 8, 16, K), BF16),
            vmem((2, 2, 16, K), F32),
            vmem((2, 8, 16, K), F32),
            pltpu.SemaphoreType.DMA((2,)),
            pltpu.SemaphoreType.DMA((7, 2)),
            pltpu.SemaphoreType.DMA((2, 4, 2)),
            pltpu.SemaphoreType.DMA((2, 6, 2)),
            pltpu.SemaphoreType.DMA((8, 2)),
        ],
        compiler_params=pltpu.CompilerParams(
            collective_id=0, has_side_effects=True, vmem_limit_bytes=48 * 1024 * 1024
        ),
        name="range_finder",
    )(activations, probe_matrix)
    return first_t.T, second_t.T


def solution(mesh):
    return jax.shard_map(
        on_device,
        mesh=mesh,
        in_specs=(P(("grp", "row"), None), P(None, "row")),
        out_specs=(P(None, ("grp", "row")), P(None, "row")),
        check_vma=False,
    )
```

```python
import jax
import jax.numpy as jnp
from jax import lax
from jax.experimental import pallas as pl
from jax.experimental.pallas import tpu as pltpu
from jax.sharding import PartitionSpec as P

MESH = pl.DeviceIdType.MESH
NX, NY, NZ = 4, 8, 8
ROW = 2 * NZ
K = 128
TOK = 512
D = 4096
F32, BF16 = jnp.float32, jnp.bfloat16
NT = (((1,), (1,)), ((), ()))


def each(low, high, body):
    def step(i, carry):
        body(i)
        return carry

    lax.fori_loop(low, high, step, 0)


def kernel(
    act_hbm, probe_hbm, out_first, out_second,
    act, p_own, p_rel, q_own, q_rel, acc_t, sk,
    g_loc, g_r1, g_s1, g_r2, g_s2, g_r3, g_full, elim_g, elim_x, linv,
    sib_out, sib_in, part, s1, r1a, r1b, t0, t1, r2, u, r3,
    bt, first, second,
    in_sem, probe_sem, gram_sem, cross_sem, sib_sem, gather_sem, line_sem, pass_sem,
):
    grp, row = lax.axis_index("grp"), lax.axis_index("row")
    y, x = lax.div(grp, NX), lax.rem(grp, NX)
    z, c = lax.div(row, 2), lax.rem(row, 2)

    def z_dev(d):
        return (grp, lax.rem(z + d, NZ) * 2 + c)

    def y_dev(d):
        return (lax.rem(y + d, NY) * NX + x, row)

    def x_dev(d):
        return (y * NX + lax.rem(x + d, NX), row)

    def r_dev(d):
        return (grp, lax.rem(row + d, ROW))

    sib = (grp, row + 1 - 2 * c)

    def send(src, dst, sems, dev):
        pltpu.make_async_remote_copy(
            src_ref=src, dst_ref=dst, send_sem=sems.at[0], recv_sem=sems.at[1],
            device_id=dev, device_id_type=MESH,
        ).start()

    sent = []

    def arrived(ref, sems):
        pltpu.make_async_copy(ref, ref, sems.at[1]).wait()
        sent.append((ref, sems))

    load_act = pltpu.make_async_copy(act_hbm, act, in_sem.at[0])
    load_probe = pltpu.make_async_copy(probe_hbm, p_own, in_sem.at[1])
    load_probe.start()
    load_act.start()

    barrier = pltpu.get_barrier_semaphore()

    def greet(dev):
        pl.semaphore_signal(barrier, inc=1, device_id=dev, device_id_type=MESH)

    each(1, ROW, lambda d: greet(r_dev(d)))
    each(1, NY, lambda d: greet(y_dev(d)))
    each(1, NX, lambda d: greet(x_dev(d)))
    load_probe.wait()
    pl.semaphore_wait(barrier, ROW - 1 + NY - 1 + NX - 1)

    rows_y = pl.ds(pl.multiple_of(lax.rem(y, 4) * 32, 32), 32)
    rows_x = pl.ds(pl.multiple_of(x * 32, 32), 32)
    low, high = pl.ds(0, 128), pl.ds(128, 128)

    def probe_z(d):
        send(p_own.at[rows_y, low], p_rel.at[7 - d, rows_y, low], probe_sem.at[0], z_dev(d))
        send(p_own.at[rows_x, high], p_rel.at[7 - d, rows_x, high], probe_sem.at[1], z_dev(d))

    each(1, NZ, probe_z)
    send(p_own, q_own, probe_sem.at[2], sib)

    def columns(at, width):
        return pl.ds(pl.multiple_of(at, width), width)

    def probe_dot(block, z_at, c_at):
        return lax.dot_general(
            act[:, columns((z_at * 2 + c_at) * 256, 256)], block, NT, preferred_element_type=F32
        )

    arrived(p_rel.at[:, pl.ds(0, 32), low], probe_sem.at[0])
    for d in (1, 7, 2 + 4 * c):
        send(p_rel.at[:, rows_y, low], p_rel.at[:, rows_y, low], probe_sem.at[3], y_dev(d))
    arrived(p_rel.at[:, pl.ds(0, 32), high], probe_sem.at[1])
    for d in (1, 2, 3):
        send(p_rel.at[:, rows_x, high], p_rel.at[:, rows_x, high], probe_sem.at[4], x_dev(d))
    load_act.wait()
    acc_t[...] = probe_dot(p_own[...], z, c)
    arrived(q_own, probe_sem.at[2])
    acc_t[...] += probe_dot(q_own[...], z, 1 - c)
    arrived(p_rel.at[:, pl.ds(0, 96), high], probe_sem.at[4])
    send(p_rel.at[:, :, high], q_rel.at[:, :, high], probe_sem.at[5], sib)
    arrived(p_rel.at[:, pl.ds(0, 96), low], probe_sem.at[3])
    send(p_rel.at[:, :, low], q_rel.at[:, :, low], probe_sem.at[6], sib)

    def add_own(d):
        acc_t[...] += probe_dot(p_rel[d], lax.rem(z + d + 1, NZ), c)

    def add_sib(d):
        acc_t[...] += probe_dot(q_rel[d], lax.rem(z + d + 1, NZ), 1 - c)

    each(0, NZ - 1, add_own)
    arrived(q_rel.at[:, :, high], probe_sem.at[5])
    arrived(q_rel.at[:, :, low], probe_sem.at[6])
    each(0, NZ - 1, add_sib)
    sk[...] = acc_t[...].T.astype(BF16)

    sublane = lax.broadcasted_iota(jnp.int32, (8, K), 0)

    def spread(line):
        return jnp.broadcast_to(line, (8, K))

    def block_step(left, right, at, lane):
        rows = left.shape[0]
        pivot = [spread(left[0:8, lane + j : lane + j + 1]) for j in range(8)]
        d = [[spread(pivot[j][i : i + 1, :]) if i >= j else None for j in range(8)] for i in range(8)]
        g = [spread(left[j : j + 1, :]) for j in range(8)]
        x = [spread(right[j : j + 1, :]) for j in range(8)]
        scale = []
        for k in range(8):
            scale.append(lax.rsqrt(d[k][k]))
            for i in range(k + 1, 8):
                d[i][k] = d[i][k] * scale[k]
            for j in range(k + 1, 8):
                for i in range(j, 8):
                    d[i][j] = d[i][j] - d[i][k] * d[j][k]
            g[k] = g[k] * scale[k]
            x[k] = x[k] * scale[k]
            for j in range(k + 1, 8):
                g[j] = g[j] - d[j][k] * g[k]
                x[j] = x[j] - d[j][k] * x[k]
        done = x[0]
        for k in range(1, 8):
            done = jnp.where(sublane == k, x[k], done)
        linv[pl.ds(pl.multiple_of(at * 8, 8), 8), :] = done
        for k in range(7, -1, -1):
            g[k] = g[k] * scale[k]
            x[k] = x[k] * scale[k]
            for j in range(k):
                g[j] = g[j] - d[k][j] * g[k]
                x[j] = x[j] - d[k][j] * x[k]
        groups = (rows - 8) // 8
        rest, right = left[8:, :].reshape(groups, 8, K), right[8:, :].reshape(groups, 8, K)
        below = rest
        for k in range(8):
            col = jnp.broadcast_to(below[:, :, lane + k : lane + k + 1], (groups, 8, K))
            rest = rest - col * g[k][None]
            right = right - col * x[k][None]
        return rest.reshape(rows - 8, K), right.reshape(rows - 8, K)

    def eliminate(rows, start):
        def step(i, carry):
            left, right = elim_g[0:rows, :], elim_x[0:rows, :]
            left, right = block_step(left, right, start + 2 * i, 0)
            left, right = block_step(left, right, start + 2 * i + 1, 8)
            elim_g[0 : rows - 16, :] = pltpu.roll(left, K - 16, 1)
            elim_x[0 : rows - 16, :] = right
            return carry

        lax.fori_loop(0, 2, step, 0)

    def solve_round(rd, a_at, b_at, a_dev, b_dev):
        gram = gram_sem.at[rd]
        cross = cross_sem.at[rd]
        sketch = sk[...]
        g_loc[rd] = lax.dot_general(sketch, sketch, NT, preferred_element_type=F32).reshape(ROW, 8, K)
        each(1, ROW, lambda d: send(
            g_loc.at[rd, lax.rem(row + d, ROW)], g_r1.at[rd, d - 1], gram.at[0], r_dev(d)))

        def for_sibling(d):
            a = lax.rem(a_at + d, 8)
            term = jnp.dot(
                sk[...], act[:, columns(a * 512 + (1 - c) * 256, 256)], preferred_element_type=F32
            )
            sib_out[rd, d - 1] = term.T.astype(BF16)
            send(sib_out.at[rd, d - 1], sib_in.at[rd, d - 1], sib_sem.at[rd, d - 1], sib)

        def for_self(d):
            a = lax.rem(a_at + d, 8)
            term = jnp.dot(
                sk[...], act[:, columns(a * 512 + c * 256, 256)], preferred_element_type=F32
            ).T
            pltpu.make_async_copy(sib_in.at[rd, 0], sib_in.at[rd, 0], sib_sem.at[rd, d - 1, 1]).wait()
            both = (term + sib_in[rd, d - 1].astype(F32)).reshape(2, 8, 16, K)
            part[d - 1] = both
            s1[rd, d - 1] = both.astype(BF16)

        def for_other(d):
            for_self(d)
            send(s1.at[rd, d - 1, 0], r1a.at[rd, d - 1], cross.at[1], a_dev(d))

        def along_b(half):
            each(1, 8, lambda d: send(
                s1.at[rd, pl.ds(4 * half, 4), 1, lax.rem(b_at + d, 8)],
                r1b.at[rd, half, d - 1], cross.at[6 * half], b_dev(d)))

        each(1, 9, for_sibling)
        arrived(g_r1.at[rd], gram.at[0])
        total = g_loc[rd, row]
        for d in range(ROW - 1):
            total = total + g_r1[rd, d]
        g_s1[rd] = total
        each(1, NY, lambda d: send(g_s1.at[rd], g_r2.at[rd, d - 1], gram.at[1], y_dev(d)))
        each(1, 5, for_other)
        along_b(0)
        arrived(g_r2.at[rd], gram.at[1])
        for d in range(NY - 1):
            total = total + g_r2[rd, d]
        g_s2[rd] = total
        each(1, NX, lambda d: send(g_s2.at[rd], g_r3.at[rd, d - 1], gram.at[2], x_dev(d)))
        each(5, 8, for_other)
        for_self(8)
        along_b(1)
        arrived(g_r3.at[rd], gram.at[2])
        for d in range(NX - 1):
            total = total + g_r3[rd, d]
        g_full[rd, row] = total
        each(1, ROW, lambda d: send(g_full.at[rd, row], g_full.at[rd, row], gram.at[3], r_dev(d)))

        arrived(g_full.at[rd, pl.ds(0, ROW - 1)], gram.at[3])
        elim_g[...] = g_full[rd].reshape(K, K)
        elim_x[...] = (
            lax.broadcasted_iota(jnp.int32, (K, K), 0) == lax.broadcasted_iota(jnp.int32, (K, K), 1)
        ).astype(F32)
        eliminate(128, 0)
        eliminate(96, 4)

        arrived(r1a.at[rd], cross.at[1])
        total_0 = part[7, 0]
        for d in range(7):
            total_0 = total_0 + r1a[rd, d].astype(F32)
        t0[rd] = total_0
        each(1, 8, lambda d: send(
            t0.at[rd, lax.rem(b_at + d, 8)], r2.at[rd, 0, d - 1], cross.at[3], b_dev(d)))
        for half in range(2):
            arrived(r1b.at[rd, half], cross.at[6 * half])
            total_1 = part[4 * half : 4 * half + 4, 1, b_at]
            for d in range(7):
                total_1 = total_1 + r1b[rd, half, d].astype(F32)
            t1[rd, 4 * half : 4 * half + 4] = total_1
        each(1, 8, lambda d: send(
            t1.at[rd, d - 1], r2.at[rd, 1, d - 1], cross.at[4], a_dev(d)))
        eliminate(64, 8)
        arrived(r2.at[rd, 0], cross.at[3])
        arrived(r2.at[rd, 1], cross.at[4])
        sum_0, sum_1 = t0[rd, b_at], t1[rd, 7]
        for d in range(7):
            sum_0 = sum_0 + r2[rd, 0, d]
            sum_1 = sum_1 + r2[rd, 1, d]
        u[rd, 0] = sum_0
        u[rd, 1] = sum_1
        each(1, NX, lambda d: send(u.at[rd], r3.at[rd, d - 1], cross.at[5], x_dev(d)))
        eliminate(32, 12)
        arrived(r3.at[rd], cross.at[5])
        whole = u[rd]
        for d in range(NX - 1):
            whole = whole + r3[rd, d]
        solved = lax.dot_general(
            whole.reshape(32, K), linv[...], NT, precision=lax.Precision.HIGHEST,
            preferred_element_type=F32,
        )
        return solved.reshape(2, 16, K)

    solved = solve_round(0, y, z, y_dev, z_dev)
    first[c] = solved
    for h in range(2):
        bt[y, 2 * c + h, z] = solved[h].astype(BF16)
    each(1, NZ, lambda d: send(bt.at[y, 2 * c, z], bt.at[y, 2 * c, z], gather_sem.at[0], z_dev(d)))
    each(1, NY, lambda d: send(bt.at[y, 2 * c + 1, z], bt.at[y, 2 * c + 1, z], gather_sem.at[1], y_dev(d)))
    arrived(bt.at[0, 0, pl.ds(0, 7)], gather_sem.at[0])
    each(1, NY, lambda d: send(bt.at[y, 2 * c], bt.at[y, 2 * c], line_sem.at[0, d - 1], y_dev(NY - d)))
    send(bt.at[y, 2 * c], bt.at[y, 2 * c], pass_sem.at[0, 7], sib)
    arrived(bt.at[0, 0, pl.ds(0, 7)], gather_sem.at[1])
    each(1, NZ, lambda d: send(
        bt.at[:, 2 * c + 1, z], bt.at[:, 2 * c + 1, z], line_sem.at[1, d - 1], z_dev(NZ - d)))
    send(bt.at[:, 2 * c + 1, z], bt.at[:, 2 * c + 1, z], pass_sem.at[1, 7], sib)
    send(first.at[c], first.at[c], gather_sem.at[6], sib)
    piece = bt.at[0, 0]

    def forward(d):
        pltpu.make_async_copy(piece, piece, line_sem.at[0, d - 1, 1]).wait()
        at_y = bt.at[lax.rem(y + d, NY), 2 * c]
        send(at_y, at_y, pass_sem.at[0, d - 1], sib)
        pltpu.make_async_copy(piece, piece, line_sem.at[1, d - 1, 1]).wait()
        at_z = bt.at[:, 2 * c + 1, lax.rem(z + d, NZ)]
        send(at_z, at_z, pass_sem.at[1, d - 1], sib)

    for d in (1, 7, 2, 6, 3, 5, 4):
        forward(d)

    def back_dot(a, c_at):
        return jnp.dot(
            act[:, columns(a * 512 + c_at * 256, 256)],
            bt[a, pl.ds(2 * c_at, 2)].reshape(256, K),
            preferred_element_type=F32,
        )

    acc_t[...] = back_dot(0, c)

    def add_back(c_at):
        def add(a):
            acc_t[...] += back_dot(a, c_at)

        return add

    each(1, 8, add_back(c))

    def passed(d):
        pltpu.make_async_copy(piece, piece, pass_sem.at[0, d, 1]).wait()
        pltpu.make_async_copy(piece, piece, pass_sem.at[1, d, 1]).wait()

    each(0, 8, passed)
    each(0, 8, add_back(1 - c))
    sk[...] = acc_t[...].T.astype(BF16)

    solved = solve_round(1, z, y, z_dev, y_dev)
    second[:, y] = solved
    each(1, NY, lambda d: send(second.at[:, y], second.at[:, y], gather_sem.at[7], y_dev(d)))
    arrived(first.at[0], gather_sem.at[6])
    out_first[...] = first[lax.div(x, 2), lax.rem(x, 2), pl.ds(pl.multiple_of(8 * c, 8), 8), :]
    arrived(second.at[:, pl.ds(0, 7)], gather_sem.at[7])
    out_second[...] = second[...].reshape(256, K)
    for ref, sems in sent:
        pltpu.make_async_copy(ref, ref, sems.at[0]).wait()

    def left_behind(d):
        for i in range(2):
            pltpu.make_async_copy(sib_in.at[i, 0], sib_in.at[i, 0], sib_sem.at[i, d, 0]).wait()
            pltpu.make_async_copy(piece, piece, pass_sem.at[i, d, 0]).wait()

    each(0, 8, left_behind)

    def line_left(d):
        for i in range(2):
            pltpu.make_async_copy(piece, piece, line_sem.at[i, d, 0]).wait()

    each(0, 7, line_left)


def on_device(activations, probe_matrix):
    vmem = pltpu.VMEM
    first_t, second_t = pl.pallas_call(
        kernel,
        out_shape=(
            jax.ShapeDtypeStruct((8, K), F32),
            jax.ShapeDtypeStruct((256, K), F32),
        ),
        in_specs=[pl.BlockSpec(memory_space=pltpu.HBM)] * 2,
        out_specs=(
            pl.BlockSpec(memory_space=pltpu.VMEM),
            pl.BlockSpec(memory_space=pltpu.VMEM),
        ),
        scratch_shapes=[
            vmem((TOK, D), BF16),
            vmem((K, 256), BF16),
            vmem((7, K, 256), BF16),
            vmem((K, 256), BF16),
            vmem((7, K, 256), BF16),
            vmem((TOK, K), F32),
            vmem((K, TOK), BF16),
            vmem((2, ROW, 8, K), F32),
            vmem((2, ROW - 1, 8, K), F32),
            vmem((2, 8, K), F32),
            vmem((2, NY - 1, 8, K), F32),
            vmem((2, 8, K), F32),
            vmem((2, NX - 1, 8, K), F32),
            vmem((2, ROW, 8, K), F32),
            vmem((K, K), F32),
            vmem((K, K), F32),
            vmem((K, K), F32),
            vmem((2, 8, 256, K), BF16),
            vmem((2, 8, 256, K), BF16),
            vmem((8, 2, 8, 16, K), F32),
            vmem((2, 8, 2, 8, 16, K), BF16),
            vmem((2, 7, 8, 16, K), BF16),
            vmem((2, 2, 7, 4, 16, K), BF16),
            vmem((2, 8, 16, K), F32),
            vmem((2, 8, 16, K), F32),
            vmem((2, 2, 7, 16, K), F32),
            vmem((2, 2, 16, K), F32),
            vmem((2, NX - 1, 2, 16, K), F32),
            vmem((8, 4, 8, 16, K), BF16),
            vmem((2, 2, 16, K), F32),
            vmem((2, 8, 16, K), F32),
            pltpu.SemaphoreType.DMA((2,)),
            pltpu.SemaphoreType.DMA((7, 2)),
            pltpu.SemaphoreType.DMA((2, 4, 2)),
            pltpu.SemaphoreType.DMA((2, 7, 2)),
            pltpu.SemaphoreType.DMA((2, 8, 2)),
            pltpu.SemaphoreType.DMA((8, 2)),
            pltpu.SemaphoreType.DMA((2, 7, 2)),
            pltpu.SemaphoreType.DMA((2, 8, 2)),
        ],
        compiler_params=pltpu.CompilerParams(
            collective_id=0, has_side_effects=True, vmem_limit_bytes=58 * 1024 * 1024
        ),
        name="range_finder",
    )(activations, probe_matrix)
    return first_t.T, second_t.T


def solution(mesh):
    return jax.shard_map(
        on_device,
        mesh=mesh,
        in_specs=(P(("grp", "row"), None), P(None, "row")),
        out_specs=(P(None, ("grp", "row")), P(None, "row")),
        check_vma=False,
    )
```

```python
import jax
import jax.numpy as jnp
from jax import lax
from jax.experimental import pallas as pl
from jax.experimental.pallas import tpu as pltpu
from jax.sharding import PartitionSpec as P

MESH = pl.DeviceIdType.MESH
NX, NY, NZ = 4, 8, 8
K = 128
TOK = 512
D = 4096
F32, BF16 = jnp.float32, jnp.bfloat16
NT = (((1,), (1,)), ((), ()))


def each(low, high, body):
    def step(i, carry):
        body(i)
        return carry

    lax.fori_loop(low, high, step, 0)


def kernel(
    act_hbm, probe_hbm, out_first, out_second,
    act, p_own, p_full, half_out, half_in, sk,
    g_loc, g_r1, g_r2, g_full, elim_g, elim_x, linv,
    part, s1, r1a, r1b, t0, t1, r2, r3,
    bt, first, second,
    in_sem, probe_sem, half_sem, gram_sem, cross_sem, gather_sem,
):
    grp, row = lax.axis_index("grp"), lax.axis_index("row")
    y, x = lax.div(grp, NX), lax.rem(grp, NX)
    z, c = lax.div(row, 2), lax.rem(row, 2)
    x0, x1 = lax.rem(x, 2), lax.div(x, 2)

    def z_dev(d):
        return (grp, lax.rem(z + d, NZ) * 2 + c)

    def y_dev(d):
        return (lax.rem(y + d, NY) * NX + x, row)

    def x_dev(d):
        return (y * NX + lax.rem(x + d, NX), row)

    g_at, t_at = z * 2 + x0, y * 2 + x1

    def scatter_dev(d):
        at = lax.rem(g_at + d, 16)
        return (y * NX + 2 * x1 + lax.rem(at, 2), lax.div(at, 2) * 2 + c)

    def total_dev(d):
        at = lax.rem(t_at + d, 16)
        return (lax.div(at, 2) * NX + 2 * lax.rem(at, 2) + x0, row)

    sib = (grp, row + 1 - 2 * c)

    def send(src, dst, sems, dev):
        pltpu.make_async_remote_copy(
            src_ref=src, dst_ref=dst, send_sem=sems.at[0], recv_sem=sems.at[1],
            device_id=dev, device_id_type=MESH,
        ).start()

    sent = []

    def arrived(ref, sems):
        pltpu.make_async_copy(ref, ref, sems.at[1]).wait()
        sent.append((ref, sems))

    def columns(at, width):
        return pl.ds(pl.multiple_of(at, width), width)

    rows_y = columns(lax.rem(y, 4) * 16, 16)
    rows_x = columns(64 + x * 16, 16)
    mine = columns(c * TOK, TOK)
    load_probe = pltpu.make_async_copy(probe_hbm, p_own, in_sem.at[1])
    load_probe.start()
    for rows in (rows_y, rows_x):
        pltpu.make_async_copy(probe_hbm.at[rows], p_full.at[rows, columns(z * 256, 256)], in_sem.at[2]).start()

    def load(a):
        pltpu.make_async_copy(
            act_hbm.at[:, columns(a * 512 + c * 256, 256)], act.at[mine, columns(a * 256, 256)], in_sem.at[0]
        ).start()

    each(0, 8, load)

    barrier = pltpu.get_barrier_semaphore()

    def greet(dev):
        pl.semaphore_signal(barrier, inc=1, device_id=dev, device_id_type=MESH)

    each(1, 16, lambda d: greet(scatter_dev(d)))
    each(1, 16, lambda d: greet(total_dev(d)))
    greet((y * NX + 3 - x, row))
    greet(sib)
    load_probe.wait()
    pl.semaphore_wait(barrier, 32)

    def probe_z(d):
        for rows, sems in ((rows_y, probe_sem.at[0]), (rows_x, probe_sem.at[1])):
            send(p_own.at[rows], p_full.at[rows, columns(z * 256, 256)], sems, z_dev(d))

    each(1, NZ, probe_z)

    def push(a):
        send(
            act_hbm.at[:, columns(a * 512 + (1 - c) * 256, 256)],
            act.at[mine, columns(a * 256, 256)], probe_sem.at[2], sib)

    each(0, 8, push)
    two = p_full.at[pl.ds(0, 32), pl.ds(0, 256)]
    pltpu.make_async_copy(two, two, in_sem.at[2]).wait()
    seven = p_full.at[pl.ds(0, 16), pl.ds(0, 7 * 256)]
    arrived(seven, probe_sem.at[0])
    for d in (1, 7, 2 + 4 * c):
        send(p_full.at[rows_y], p_full.at[rows_y], probe_sem.at[3], y_dev(d))
    arrived(seven, probe_sem.at[1])
    for d in (1, 2, 3):
        send(p_full.at[rows_x], p_full.at[rows_x], probe_sem.at[4], x_dev(d))
    own_half = act.at[pl.ds(0, TOK)]
    pltpu.make_async_copy(own_half, own_half, in_sem.at[0]).wait()
    arrived(own_half, probe_sem.at[2])
    arrived(p_full.at[pl.ds(0, 48)], probe_sem.at[3])
    arrived(p_full.at[pl.ds(0, 48)], probe_sem.at[4])

    def both_halves(rd, product):
        def partial(q):
            half_out[rd, q] = product(act[columns(q * 256, 256), :])
            send(half_out.at[rd, q], half_in.at[rd, q], half_sem.at[rd, q], sib)

        each(0, 4, partial)
        for q in range(4):
            arrived(half_in.at[rd, q], half_sem.at[rd, q])
            sk[:, q * 256 : q * 256 + 256] = (half_out[rd, q] + half_in[rd, q]).T.astype(BF16)

    both_halves(0, lambda rows: lax.dot_general(rows, p_full[...], NT, preferred_element_type=F32))

    sublane = lax.broadcasted_iota(jnp.int32, (8, K), 0)

    def spread(line):
        return jnp.broadcast_to(line, (8, K))

    def block_step(left, right, at, lane):
        rows = left.shape[0]
        pivot = [spread(left[0:8, lane + j : lane + j + 1]) for j in range(8)]
        d = [[spread(pivot[j][i : i + 1, :]) if i >= j else None for j in range(8)] for i in range(8)]
        g = [spread(left[j : j + 1, :]) for j in range(8)]
        x = [spread(right[j : j + 1, :]) for j in range(8)]
        scale = []
        for k in range(8):
            scale.append(lax.rsqrt(d[k][k]))
            for i in range(k + 1, 8):
                d[i][k] = d[i][k] * scale[k]
            for j in range(k + 1, 8):
                for i in range(j, 8):
                    d[i][j] = d[i][j] - d[i][k] * d[j][k]
            g[k] = g[k] * scale[k]
            x[k] = x[k] * scale[k]
            for j in range(k + 1, 8):
                g[j] = g[j] - d[j][k] * g[k]
                x[j] = x[j] - d[j][k] * x[k]
        done = x[0]
        for k in range(1, 8):
            done = jnp.where(sublane == k, x[k], done)
        linv[pl.ds(pl.multiple_of(at * 8, 8), 8), :] = done
        for k in range(7, -1, -1):
            g[k] = g[k] * scale[k]
            x[k] = x[k] * scale[k]
            for j in range(k):
                g[j] = g[j] - d[k][j] * g[k]
                x[j] = x[j] - d[k][j] * x[k]
        groups = (rows - 8) // 8
        rest, right = left[8:, :].reshape(groups, 8, K), right[8:, :].reshape(groups, 8, K)
        below = rest
        for k in range(8):
            col = jnp.broadcast_to(below[:, :, lane + k : lane + k + 1], (groups, 8, K))
            rest = rest - col * g[k][None]
            right = right - col * x[k][None]
        return rest.reshape(rows - 8, K), right.reshape(rows - 8, K)

    def eliminate(rows, start):
        def step(i, carry):
            left, right = elim_g[0:rows, :], elim_x[0:rows, :]
            left, right = block_step(left, right, start + 2 * i, 0)
            left, right = block_step(left, right, start + 2 * i + 1, 8)
            elim_g[0 : rows - 16, :] = pltpu.roll(left, K - 16, 1)
            elim_x[0 : rows - 16, :] = right
            return carry

        lax.fori_loop(0, 2, step, 0)

    def solve_round(rd, a_at, b_at, a_dev, b_dev):
        gram = gram_sem.at[rd]
        cross = cross_sem.at[rd]
        sketch = sk[...]
        g_loc[rd] = lax.dot_general(sketch, sketch, NT, preferred_element_type=F32).reshape(16, 8, K)
        each(1, 16, lambda d: send(
            g_loc.at[rd, lax.rem(g_at + d, 16)], g_r1.at[rd, d - 1], gram.at[0], scatter_dev(d)))

        def cross_of(d):
            a = lax.rem(a_at + d, 8)
            term = jnp.dot(sk[...], act[:, columns(a * 256, 256)], preferred_element_type=F32)
            term = term.T.reshape(2, 8, 16, K)
            part[d - 1] = term
            s1[rd, d - 1] = term.astype(BF16)

        def cross_to(d):
            cross_of(d)
            send(s1.at[rd, d - 1, 0], r1a.at[rd, d - 1], cross.at[1], a_dev(d))

        def along_b(half):
            each(1, 8, lambda d: send(
                s1.at[rd, pl.ds(4 * half, 4), 1, lax.rem(b_at + d, 8)],
                r1b.at[rd, half, d - 1], cross.at[2 * half], b_dev(d)))

        each(1, 5, cross_to)
        arrived(g_r1.at[rd], gram.at[0])
        total = g_loc[rd, g_at]
        for d in range(15):
            total = total + g_r1[rd, d]
        g_r2[rd, t_at] = total
        each(1, 16, lambda d: send(g_r2.at[rd, t_at], g_r2.at[rd, t_at], gram.at[1], total_dev(d)))
        along_b(0)
        each(5, 8, cross_to)
        cross_of(8)
        arrived(g_r2.at[rd, pl.ds(0, 15)], gram.at[1])
        total = g_r2[rd, 0]
        for d in range(1, 16):
            total = total + g_r2[rd, d]
        g_full[rd, g_at] = total
        each(1, 16, lambda d: send(
            g_full.at[rd, g_at], g_full.at[rd, g_at], gram.at[2], scatter_dev(d)))
        along_b(1)

        arrived(g_full.at[rd, pl.ds(0, 15)], gram.at[2])
        elim_g[...] = g_full[rd].reshape(K, K)
        elim_x[...] = (
            lax.broadcasted_iota(jnp.int32, (K, K), 0) == lax.broadcasted_iota(jnp.int32, (K, K), 1)
        ).astype(F32)
        eliminate(128, 0)
        eliminate(96, 4)

        arrived(r1a.at[rd], cross.at[1])
        total_0 = part[7, 0]
        for d in range(7):
            total_0 = total_0 + r1a[rd, d].astype(F32)
        t0[rd] = total_0
        each(1, 8, lambda d: send(
            t0.at[rd, lax.rem(b_at + d, 8)], r2.at[rd, 0, d - 1], cross.at[3], b_dev(d)))
        for half in range(2):
            arrived(r1b.at[rd, half], cross.at[2 * half])
            total_1 = part[4 * half : 4 * half + 4, 1, b_at]
            for d in range(7):
                total_1 = total_1 + r1b[rd, half, d].astype(F32)
            t1[rd, 4 * half : 4 * half + 4] = total_1
        each(1, 8, lambda d: send(
            t1.at[rd, d - 1], r2.at[rd, 1, d - 1], cross.at[4], a_dev(d)))
        eliminate(64, 8)
        arrived(r2.at[rd, 0], cross.at[3])
        arrived(r2.at[rd, 1], cross.at[4])
        sum_0, sum_1 = t0[rd, b_at], t1[rd, 7]
        for d in range(7):
            sum_0 = sum_0 + r2[rd, 0, d]
            sum_1 = sum_1 + r2[rd, 1, d]
        r3[rd, x, 0] = sum_0
        r3[rd, x, 1] = sum_1
        each(1, NX, lambda d: send(r3.at[rd, x], r3.at[rd, x], cross.at[5], x_dev(d)))
        eliminate(32, 12)
        arrived(r3.at[rd, pl.ds(0, NX - 1)], cross.at[5])
        whole = r3[rd, 0]
        for d in range(1, NX):
            whole = whole + r3[rd, d]
        solved = lax.dot_general(
            whole.reshape(32, K), linv[...], NT, precision=lax.Precision.HIGHEST,
            preferred_element_type=F32,
        )
        return solved.reshape(2, 16, K)

    solved = solve_round(0, y, z, y_dev, z_dev)
    first[c] = solved
    for h in range(2):
        bt[y, h, z] = solved[h].astype(BF16)
    each(1, NZ, lambda d: send(bt.at[y, 0, z], bt.at[y, 0, z], gather_sem.at[0], z_dev(d)))
    each(1, NY, lambda d: send(bt.at[y, 1, z], bt.at[y, 1, z], gather_sem.at[1], y_dev(d)))
    arrived(bt.at[0, 0, pl.ds(0, 7)], gather_sem.at[0])
    each(1, NY, lambda d: send(bt.at[y, 0], bt.at[y, 0], gather_sem.at[2], y_dev(d)))
    arrived(bt.at[pl.ds(0, 7), 0, 0], gather_sem.at[1])
    each(1, NZ, lambda d: send(bt.at[:, 1, z], bt.at[:, 1, z], gather_sem.at[3], z_dev(d)))
    send(first.at[c], first.at[c], gather_sem.at[4], sib)
    arrived(bt.at[pl.ds(0, 7), 0], gather_sem.at[2])
    arrived(bt.at[:, 0, pl.ds(0, 7)], gather_sem.at[3])
    both_halves(1, lambda rows: jnp.dot(
        rows, bt[...].reshape(2048, K), preferred_element_type=F32))

    solved = solve_round(1, z, y, z_dev, y_dev)
    second[:, y] = solved
    each(1, NY, lambda d: send(second.at[:, y], second.at[:, y], gather_sem.at[5], y_dev(d)))
    arrived(first.at[0], gather_sem.at[4])
    out_first[...] = first[lax.div(x, 2), lax.rem(x, 2), pl.ds(pl.multiple_of(8 * c, 8), 8), :]
    arrived(second.at[:, pl.ds(0, 7)], gather_sem.at[5])
    out_second[...] = second[...].reshape(256, K)
    for ref, sems in sent:
        pltpu.make_async_copy(ref, ref, sems.at[0]).wait()


def on_device(activations, probe_matrix):
    vmem = pltpu.VMEM
    first_t, second_t = pl.pallas_call(
        kernel,
        out_shape=(
            jax.ShapeDtypeStruct((8, K), F32),
            jax.ShapeDtypeStruct((256, K), F32),
        ),
        in_specs=[pl.BlockSpec(memory_space=pltpu.HBM)] * 2,
        out_specs=(
            pl.BlockSpec(memory_space=pltpu.VMEM),
            pl.BlockSpec(memory_space=pltpu.VMEM),
        ),
        scratch_shapes=[
            vmem((2 * TOK, D // 2), BF16),
            vmem((K, 256), BF16),
            vmem((K, D // 2), BF16),
            vmem((2, 4, 256, K), F32),
            vmem((2, 4, 256, K), F32),
            vmem((K, 2 * TOK), BF16),
            vmem((2, 16, 8, K), F32),
            vmem((2, 15, 8, K), F32),
            vmem((2, 16, 8, K), F32),
            vmem((2, 16, 8, K), F32),
            vmem((K, K), F32),
            vmem((K, K), F32),
            vmem((K, K), F32),
            vmem((8, 2, 8, 16, K), F32),
            vmem((2, 8, 2, 8, 16, K), BF16),
            vmem((2, 7, 8, 16, K), BF16),
            vmem((2, 2, 7, 4, 16, K), BF16),
            vmem((2, 8, 16, K), F32),
            vmem((2, 8, 16, K), F32),
            vmem((2, 2, 7, 16, K), F32),
            vmem((2, NX, 2, 16, K), F32),
            vmem((8, 2, 8, 16, K), BF16),
            vmem((2, 2, 16, K), F32),
            vmem((2, 8, 16, K), F32),
            pltpu.SemaphoreType.DMA((3,)),
            pltpu.SemaphoreType.DMA((5, 2)),
            pltpu.SemaphoreType.DMA((2, 4, 2)),
            pltpu.SemaphoreType.DMA((2, 3, 2)),
            pltpu.SemaphoreType.DMA((2, 6, 2)),
            pltpu.SemaphoreType.DMA((6, 2)),
        ],
        compiler_params=pltpu.CompilerParams(
            collective_id=0, has_side_effects=True, vmem_limit_bytes=58 * 1024 * 1024
        ),
        name="range_finder",
    )(activations, probe_matrix)
    return first_t.T, second_t.T


def solution(mesh):
    return jax.shard_map(
        on_device,
        mesh=mesh,
        in_specs=(P(("grp", "row"), None), P(None, "row")),
        out_specs=(P(None, ("grp", "row")), P(None, "row")),
        check_vma=False,
    )
```

```python
import jax
import jax.numpy as jnp
from jax import lax
from jax.experimental import pallas as pl
from jax.experimental.pallas import tpu as pltpu
from jax.sharding import PartitionSpec as P

MESH = pl.DeviceIdType.MESH
NX, NY, NZ = 4, 8, 8
K = 128
TOK = 512
D = 4096
F32, BF16 = jnp.float32, jnp.bfloat16
NT = (((1,), (1,)), ((), ()))
FAR = (4, 3, 5, 2, 6, 1, 7)


def each(low, high, body):
    def step(i, carry):
        body(i)
        return carry

    lax.fori_loop(low, high, step, 0)


def kernel(
    act_hbm, probe_hbm, out_first, out_second,
    act, p_in, p_own, p_line, p_full, half_out, half_in, sk,
    g_loc, g_r1, g_r2, g_r3, g_full, elim_g, elim_x, linv,
    part, s1, r1a, r1b, t0, t1, r2, r3,
    bt, first, second,
    in_sem, probe_sem, half_sem, gram_sem, cross_sem, gather_sem,
):
    grp, row = lax.axis_index("grp"), lax.axis_index("row")
    y, x = lax.div(grp, NX), lax.rem(grp, NX)
    z, c = lax.div(row, 2), lax.rem(row, 2)

    def z_dev(d):
        return (grp, lax.rem(z + d, NZ) * 2 + c)

    def y_dev(d):
        return (lax.rem(y + d, NY) * NX + x, row)

    def x_dev(d):
        return (y * NX + lax.rem(x + d, NX), row)

    sib = (grp, row + 1 - 2 * c)

    def send(src, dst, sems, dev):
        pltpu.make_async_remote_copy(
            src_ref=src, dst_ref=dst, send_sem=sems.at[0], recv_sem=sems.at[1],
            device_id=dev, device_id_type=MESH,
        ).start()

    sent = []

    def arrived(ref, sems):
        pltpu.make_async_copy(ref, ref, sems.at[1]).wait()
        sent.append((ref, sems))

    def columns(at, width):
        return pl.ds(pl.multiple_of(at, width), width)

    mine = columns(c * TOK, TOK)
    load_probe = pltpu.make_async_copy(probe_hbm, p_in, in_sem.at[1])
    load_probe.start()

    def load(a):
        pltpu.make_async_copy(
            act_hbm.at[:, columns(a * 512 + c * 256, 256)], act.at[mine, columns(a * 256, 256)], in_sem.at[0]
        ).start()

    each(0, 8, load)

    barrier = pltpu.get_barrier_semaphore()

    def greet(dev):
        pl.semaphore_signal(barrier, inc=1, device_id=dev, device_id_type=MESH)

    for d in (4, 3, 5, 2, 6, 1, 7):
        greet(z_dev(d))
        greet(y_dev(d))
    for d in (2, 1, 3):
        greet(x_dev(d))
    greet(sib)
    load_probe.wait()
    p_own[...] = p_in[...].T.reshape(2, 4, 32, K)
    y_part = lax.rem(y, 4)
    p_line[z, 0] = p_own[0, y_part]
    p_line[z, 1] = p_own[1, x]
    pl.semaphore_wait(barrier, 18)

    for d in (4, 3, 5, 2, 6, 1, 7):
        send(p_line.at[z], p_line.at[z], probe_sem.at[0], z_dev(d))

    def push(a):
        send(
            act_hbm.at[:, columns(a * 512 + (1 - c) * 256, 256)],
            act.at[mine, columns(a * 256, 256)], probe_sem.at[2], sib)

    each(0, 8, push)
    arrived(p_line.at[pl.ds(0, 7)], probe_sem.at[0])
    for d in (1, 7, 2 + 4 * c):
        send(p_line.at[:, 0], p_full.at[:, 0, y_part], probe_sem.at[3], y_dev(d))
    for d in (2, 1, 3):
        send(p_line.at[:, 1], p_full.at[:, 1, x], probe_sem.at[4], x_dev(d))
    p_full[:, 0, y_part] = p_line[:, 0]
    p_full[:, 1, x] = p_line[:, 1]
    own_half = act.at[pl.ds(0, TOK)]
    pltpu.make_async_copy(own_half, own_half, in_sem.at[0]).wait()
    arrived(own_half, probe_sem.at[2])
    arrived(p_full.at[:, 0, pl.ds(0, 3)], probe_sem.at[3])
    arrived(p_full.at[:, 0, pl.ds(0, 3)], probe_sem.at[4])

    def both_halves(rd, product):
        def partial(q):
            half_out[rd, q] = product(act[columns(q * 256, 256), :])
            send(half_out.at[rd, q], half_in.at[rd, q], half_sem.at[rd, q], sib)

        each(0, 4, partial)
        for q in range(4):
            arrived(half_in.at[rd, q], half_sem.at[rd, q])
            sk[:, q * 256 : q * 256 + 256] = (half_out[rd, q] + half_in[rd, q]).T.astype(BF16)

    both_halves(0, lambda rows: jnp.dot(
        rows, p_full[...].reshape(2048, K), preferred_element_type=F32))

    sublane = lax.broadcasted_iota(jnp.int32, (8, K), 0)

    def spread(line):
        return jnp.broadcast_to(line, (8, K))

    def block_step(left, right, at):
        rows, lane = left.shape[0], at * 8
        pivot = [spread(left[0:8, lane + j : lane + j + 1]) for j in range(8)]
        d = [[spread(pivot[j][i : i + 1, :]) if i >= j else None for j in range(8)] for i in range(8)]
        g = [spread(left[j : j + 1, :]) for j in range(8)]
        x = [spread(right[j : j + 1, :]) for j in range(8)]
        scale = []
        for k in range(8):
            scale.append(lax.rsqrt(d[k][k]))
            for i in range(k + 1, 8):
                d[i][k] = d[i][k] * scale[k]
            for j in range(k + 1, 8):
                for i in range(j, 8):
                    d[i][j] = d[i][j] - d[i][k] * d[j][k]
            g[k] = g[k] * scale[k]
            x[k] = x[k] * scale[k]
            for j in range(k + 1, 8):
                g[j] = g[j] - d[j][k] * g[k]
                x[j] = x[j] - d[j][k] * x[k]
        done = x[0]
        for k in range(1, 8):
            done = jnp.where(sublane == k, x[k], done)
        linv[at * 8 : at * 8 + 8, :] = done
        if rows == 8:
            return None, None
        for k in range(7, -1, -1):
            g[k] = g[k] * scale[k]
            x[k] = x[k] * scale[k]
            for j in range(k):
                g[j] = g[j] - d[k][j] * g[k]
                x[j] = x[j] - d[k][j] * x[k]
        groups = (rows - 8) // 8
        rest, right = left[8:, :].reshape(groups, 8, K), right[8:, :].reshape(groups, 8, K)
        below = rest
        for k in range(8):
            col = jnp.broadcast_to(below[:, :, lane + k : lane + k + 1], (groups, 8, K))
            rest = rest - col * g[k][None]
            right = right - col * x[k][None]
        return rest.reshape(rows - 8, K), right.reshape(rows - 8, K)

    def eliminate(start):
        rows = K - 8 * start
        left, right = elim_g[0:rows, :], elim_x[0:rows, :]
        for at in range(start, start + 4):
            left, right = block_step(left, right, at)
        if left is not None:
            elim_g[0 : rows - 32, :] = left
            elim_x[0 : rows - 32, :] = right

    def solve_round(rd, a_at, b_at, a_dev, b_dev):
        gram = gram_sem.at[rd]
        cross = cross_sem.at[rd]
        sketch = sk[...]
        g_loc[rd] = lax.dot_general(sketch, sketch, NT, preferred_element_type=F32).reshape(8, 16, K)
        for d in FAR:
            send(g_loc.at[rd, lax.rem(z + d, 8)], g_r1.at[rd, d - 1], gram.at[0], z_dev(d))

        def cross_of(d):
            a = lax.rem(a_at + d, 8)
            term = jnp.dot(sk[...], act[:, columns(a * 256, 256)], preferred_element_type=F32)
            term = term.T.reshape(2, 8, 16, K)
            part[d - 1] = term
            s1[rd, d - 1] = term.astype(BF16)

        def cross_to(d):
            cross_of(d)
            send(s1.at[rd, d - 1, 0], r1a.at[rd, d - 1], cross.at[1], a_dev(d))

        def along_b(half):
            each(1, 8, lambda d: send(
                s1.at[rd, pl.ds(4 * half, 4), 1, lax.rem(b_at + d, 8)],
                r1b.at[rd, half, d - 1], cross.at[2 * half], b_dev(d)))

        each(1, 5, cross_to)
        arrived(g_r1.at[rd], gram.at[0])
        total = g_loc[rd, z]
        for d in range(7):
            total = total + g_r1[rd, d]
        g_r2[rd, y] = total
        for d in FAR:
            send(g_r2.at[rd, y], g_r2.at[rd, y], gram.at[1], y_dev(d))
        each(5, 7, cross_to)
        arrived(g_r2.at[rd, pl.ds(0, 7)], gram.at[1])
        total = g_r2[rd, 0]
        for d in range(1, 8):
            total = total + g_r2[rd, d]
        g_r3[rd, x] = total
        for d in (2, 1, 3):
            send(g_r3.at[rd, x], g_r3.at[rd, x], gram.at[2], x_dev(d))
        along_b(0)
        each(7, 8, cross_to)
        cross_of(8)
        arrived(g_r3.at[rd, pl.ds(0, 3)], gram.at[2])
        total = g_r3[rd, 0]
        for d in range(1, 4):
            total = total + g_r3[rd, d]
        g_full[rd, z] = total
        for d in FAR:
            send(g_full.at[rd, z], g_full.at[rd, z], gram.at[3], z_dev(d))
        along_b(1)

        arrived(g_full.at[rd, pl.ds(0, 7)], gram.at[3])
        elim_g[...] = g_full[rd].reshape(K, K)
        elim_x[...] = (
            lax.broadcasted_iota(jnp.int32, (K, K), 0) == lax.broadcasted_iota(jnp.int32, (K, K), 1)
        ).astype(F32)
        eliminate(0)
        eliminate(4)

        arrived(r1a.at[rd], cross.at[1])
        total_0 = part[7, 0]
        for d in range(7):
            total_0 = total_0 + r1a[rd, d].astype(F32)
        t0[rd] = total_0
        each(1, 8, lambda d: send(
            t0.at[rd, lax.rem(b_at + d, 8)], r2.at[rd, 0, d - 1], cross.at[3], b_dev(d)))
        for half in range(2):
            arrived(r1b.at[rd, half], cross.at[2 * half])
            total_1 = part[4 * half : 4 * half + 4, 1, b_at]
            for d in range(7):
                total_1 = total_1 + r1b[rd, half, d].astype(F32)
            t1[rd, 4 * half : 4 * half + 4] = total_1
        each(1, 8, lambda d: send(
            t1.at[rd, d - 1], r2.at[rd, 1, d - 1], cross.at[4], a_dev(d)))
        eliminate(8)
        arrived(r2.at[rd, 0], cross.at[3])
        arrived(r2.at[rd, 1], cross.at[4])
        sum_0, sum_1 = t0[rd, b_at], t1[rd, 7]
        for d in range(7):
            sum_0 = sum_0 + r2[rd, 0, d]
            sum_1 = sum_1 + r2[rd, 1, d]
        r3[rd, x, 0] = sum_0
        r3[rd, x, 1] = sum_1
        each(1, NX, lambda d: send(r3.at[rd, x], r3.at[rd, x], cross.at[5], x_dev(d)))
        eliminate(12)
        arrived(r3.at[rd, pl.ds(0, NX - 1)], cross.at[5])
        whole = r3[rd, 0]
        for d in range(1, NX):
            whole = whole + r3[rd, d]
        solved = lax.dot_general(
            whole.reshape(32, K), linv[...], NT, precision=lax.Precision.HIGHEST,
            preferred_element_type=F32,
        )
        return solved.reshape(2, 16, K)

    solved = solve_round(0, y, z, y_dev, z_dev)
    first[c] = solved
    for h in range(2):
        bt[y, h, z] = solved[h].astype(BF16)
    each(1, NZ, lambda d: send(bt.at[y, 0, z], bt.at[y, 0, z], gather_sem.at[0], z_dev(d)))
    each(1, NY, lambda d: send(bt.at[y, 1, z], bt.at[y, 1, z], gather_sem.at[1], y_dev(d)))
    arrived(bt.at[0, 0, pl.ds(0, 7)], gather_sem.at[0])
    each(1, NY, lambda d: send(bt.at[y, 0], bt.at[y, 0], gather_sem.at[2], y_dev(d)))
    arrived(bt.at[pl.ds(0, 7), 0, 0], gather_sem.at[1])
    each(1, NZ, lambda d: send(bt.at[:, 1, z], bt.at[:, 1, z], gather_sem.at[3], z_dev(d)))
    send(first.at[c], first.at[c], gather_sem.at[4], sib)
    arrived(bt.at[pl.ds(0, 7), 0], gather_sem.at[2])
    arrived(bt.at[:, 0, pl.ds(0, 7)], gather_sem.at[3])
    both_halves(1, lambda rows: jnp.dot(
        rows, bt[...].reshape(2048, K), preferred_element_type=F32))

    solved = solve_round(1, z, y, z_dev, y_dev)
    second[:, y] = solved
    each(1, NY, lambda d: send(second.at[:, y], second.at[:, y], gather_sem.at[5], y_dev(d)))
    arrived(first.at[0], gather_sem.at[4])
    out_first[...] = first[lax.div(x, 2), lax.rem(x, 2), pl.ds(pl.multiple_of(8 * c, 8), 8), :]
    arrived(second.at[:, pl.ds(0, 7)], gather_sem.at[5])
    out_second[...] = second[...].reshape(256, K)
    for ref, sems in sent:
        pltpu.make_async_copy(ref, ref, sems.at[0]).wait()


def on_device(activations, probe_matrix):
    vmem = pltpu.VMEM
    first_t, second_t = pl.pallas_call(
        kernel,
        out_shape=(
            jax.ShapeDtypeStruct((8, K), F32),
            jax.ShapeDtypeStruct((256, K), F32),
        ),
        in_specs=[pl.BlockSpec(memory_space=pltpu.HBM)] * 2,
        out_specs=(
            pl.BlockSpec(memory_space=pltpu.VMEM),
            pl.BlockSpec(memory_space=pltpu.VMEM),
        ),
        scratch_shapes=[
            vmem((2 * TOK, D // 2), BF16),
            vmem((K, 256), BF16),
            vmem((2, 4, 32, K), BF16),
            vmem((8, 2, 32, K), BF16),
            vmem((8, 2, 4, 32, K), BF16),
            vmem((2, 4, 256, K), F32),
            vmem((2, 4, 256, K), F32),
            vmem((K, 2 * TOK), BF16),
            vmem((2, 8, 16, K), F32),
            vmem((2, 7, 16, K), F32),
            vmem((2, 8, 16, K), F32),
            vmem((2, 4, 16, K), F32),
            vmem((2, 8, 16, K), F32),
            vmem((K, K), F32),
            vmem((K, K), F32),
            vmem((K, K), F32),
            vmem((8, 2, 8, 16, K), F32),
            vmem((2, 8, 2, 8, 16, K), BF16),
            vmem((2, 7, 8, 16, K), BF16),
            vmem((2, 2, 7, 4, 16, K), BF16),
            vmem((2, 8, 16, K), F32),
            vmem((2, 8, 16, K), F32),
            vmem((2, 2, 7, 16, K), F32),
            vmem((2, NX, 2, 16, K), F32),
            vmem((8, 2, 8, 16, K), BF16),
            vmem((2, 2, 16, K), F32),
            vmem((2, 8, 16, K), F32),
            pltpu.SemaphoreType.DMA((2,)),
            pltpu.SemaphoreType.DMA((5, 2)),
            pltpu.SemaphoreType.DMA((2, 4, 2)),
            pltpu.SemaphoreType.DMA((2, 4, 2)),
            pltpu.SemaphoreType.DMA((2, 6, 2)),
            pltpu.SemaphoreType.DMA((6, 2)),
        ],
        compiler_params=pltpu.CompilerParams(
            collective_id=0, has_side_effects=True, vmem_limit_bytes=52 * 1024 * 1024
        ),
        name="range_finder",
    )(activations, probe_matrix)
    return first_t.T, second_t.T


def solution(mesh):
    return jax.shard_map(
        on_device,
        mesh=mesh,
        in_specs=(P(("grp", "row"), None), P(None, "row")),
        out_specs=(P(None, ("grp", "row")), P(None, "row")),
        check_vma=False,
    )
```

```python
import jax
import jax.numpy as jnp
from jax import lax
from jax.experimental import pallas as pl
from jax.experimental.pallas import tpu as pltpu
from jax.sharding import PartitionSpec as P

MESH = pl.DeviceIdType.MESH
NX, NY, NZ = 4, 8, 8
K = 128
TOK = 512
D = 4096
F32, BF16 = jnp.float32, jnp.bfloat16
NT = (((1,), (1,)), ((), ()))
FAR = (4, 3, 5, 2, 6, 1, 7)


def each(low, high, body):
    def step(i, carry):
        body(i)
        return carry

    lax.fori_loop(low, high, step, 0)


def kernel(
    act_hbm, probe_hbm, out_first, out_second,
    act, p_in, p_own, p_line, p_full, half_out, half_in, sk,
    g_loc, g_r1, g_r2, g_r3, g_full, elim_g, elim_x, linv,
    part, s1, r1a, r1b, t0, t1, r2, r3,
    bt, gathered, solved, first,
    in_sem, probe_sem, half_sem, gram_sem, cross_sem, gather_sem,
):
    grp, row = lax.axis_index("grp"), lax.axis_index("row")
    y, x = lax.div(grp, NX), lax.rem(grp, NX)
    z, c = lax.div(row, 2), lax.rem(row, 2)

    def z_dev(d):
        return (grp, lax.rem(z + d, NZ) * 2 + c)

    def y_dev(d):
        return (lax.rem(y + d, NY) * NX + x, row)

    def x_dev(d):
        return (y * NX + lax.rem(x + d, NX), row)

    sib = (grp, row + 1 - 2 * c)

    def send(src, dst, sems, dev):
        pltpu.make_async_remote_copy(
            src_ref=src, dst_ref=dst, send_sem=sems.at[0], recv_sem=sems.at[1],
            device_id=dev, device_id_type=MESH,
        ).start()

    sent = []

    def arrived(ref, sems):
        pltpu.make_async_copy(ref, ref, sems.at[1]).wait()
        sent.append((ref, sems))

    def columns(at, width):
        return pl.ds(pl.multiple_of(at, width), width)

    mine = columns(c * TOK, TOK)
    load_probe = pltpu.make_async_copy(probe_hbm, p_in, in_sem.at[1])
    load_probe.start()

    def load(a):
        pltpu.make_async_copy(
            act_hbm.at[:, columns(a * 512 + c * 256, 256)], act.at[mine, columns(a * 256, 256)], in_sem.at[0]
        ).start()

    each(0, 8, load)

    barrier = pltpu.get_barrier_semaphore()

    def greet(dev):
        pl.semaphore_signal(barrier, inc=1, device_id=dev, device_id_type=MESH)

    for d in (4, 3, 5, 2, 6, 1, 7):
        greet(z_dev(d))
        greet(y_dev(d))
    for d in (2, 1, 3):
        greet(x_dev(d))
    greet(sib)
    load_probe.wait()
    p_own[...] = p_in[...].T.reshape(2, 4, 32, K)
    y_part = lax.rem(y, 4)
    p_line[z, 0] = p_own[0, y_part]
    p_line[z, 1] = p_own[1, x]
    pl.semaphore_wait(barrier, 18)

    for d in (4, 3, 5, 2, 6, 1, 7):
        send(p_line.at[z], p_line.at[z], probe_sem.at[0], z_dev(d))

    def push(a):
        send(
            act_hbm.at[:, columns(a * 512 + (1 - c) * 256, 256)],
            act.at[mine, columns(a * 256, 256)], probe_sem.at[2], sib)

    each(0, 8, push)
    arrived(p_line.at[pl.ds(0, 7)], probe_sem.at[0])
    for d in (1, 7, 2 + 4 * c):
        send(p_line.at[:, 0], p_full.at[:, 0, y_part], probe_sem.at[3], y_dev(d))
    for d in (2, 1, 3):
        send(p_line.at[:, 1], p_full.at[:, 1, x], probe_sem.at[4], x_dev(d))
    p_full[:, 0, y_part] = p_line[:, 0]
    p_full[:, 1, x] = p_line[:, 1]
    own_half = act.at[pl.ds(0, TOK)]
    pltpu.make_async_copy(own_half, own_half, in_sem.at[0]).wait()
    arrived(own_half, probe_sem.at[2])
    arrived(p_full.at[:, 0, pl.ds(0, 3)], probe_sem.at[3])
    arrived(p_full.at[:, 0, pl.ds(0, 3)], probe_sem.at[4])

    def both_halves(rd, product):
        def partial(q):
            half_out[rd, q] = product(act[columns(q * TOK, TOK), :])
            send(half_out.at[rd, q], half_in.at[rd, q], half_sem.at[rd, q], sib)

        each(0, 2, partial)
        for q in range(2):
            arrived(half_in.at[rd, q], half_sem.at[rd, q])
            sk[:, q * TOK : q * TOK + TOK] = (half_out[rd, q] + half_in[rd, q]).T.astype(BF16)

    both_halves(0, lambda rows: jnp.dot(
        rows, p_full[...].reshape(2048, K), preferred_element_type=F32))

    sublane = lax.broadcasted_iota(jnp.int32, (8, K), 0)

    def spread(line):
        return jnp.broadcast_to(line, (8, K))

    def block_step(left, right, at):
        rows, lane = left.shape[0], at * 8
        pivot = [spread(left[0:8, lane + j : lane + j + 1]) for j in range(8)]
        d = [[spread(pivot[j][i : i + 1, :]) if i >= j else None for j in range(8)] for i in range(8)]
        g = [spread(left[j : j + 1, :]) for j in range(8)]
        x = [spread(right[j : j + 1, :]) for j in range(8)]
        scale = []
        for k in range(8):
            scale.append(lax.rsqrt(d[k][k]))
            for i in range(k + 1, 8):
                d[i][k] = d[i][k] * scale[k]
            for j in range(k + 1, 8):
                for i in range(j, 8):
                    d[i][j] = d[i][j] - d[i][k] * d[j][k]
            g[k] = g[k] * scale[k]
            x[k] = x[k] * scale[k]
            for j in range(k + 1, 8):
                g[j] = g[j] - d[j][k] * g[k]
                x[j] = x[j] - d[j][k] * x[k]
        done = x[0]
        for k in range(1, 8):
            done = jnp.where(sublane == k, x[k], done)
        linv[at * 8 : at * 8 + 8, :] = done
        if rows == 8:
            return None, None
        for k in range(7, -1, -1):
            g[k] = g[k] * scale[k]
            x[k] = x[k] * scale[k]
            for j in range(k):
                g[j] = g[j] - d[k][j] * g[k]
                x[j] = x[j] - d[k][j] * x[k]
        groups = (rows - 8) // 8
        rest, right = left[8:, :].reshape(groups, 8, K), right[8:, :].reshape(groups, 8, K)
        below = rest
        for k in range(8):
            col = jnp.broadcast_to(below[:, :, lane + k : lane + k + 1], (groups, 8, K))
            rest = rest - col * g[k][None]
            right = right - col * x[k][None]
        return rest.reshape(rows - 8, K), right.reshape(rows - 8, K)

    def eliminate(start):
        rows = K - 8 * start
        left, right = elim_g[0:rows, :], elim_x[0:rows, :]
        for at in range(start, start + 4):
            left, right = block_step(left, right, at)
        if left is not None:
            elim_g[0 : rows - 32, :] = left
            elim_x[0 : rows - 32, :] = right

    def solve_round(rd, a_at, b_at, a_dev, b_dev):
        gram = gram_sem.at[rd]
        cross = cross_sem.at[rd]
        sketch = sk[...]
        g_loc[rd] = lax.dot_general(sketch, sketch, NT, preferred_element_type=F32).reshape(8, 16, K)
        for d in FAR:
            send(g_loc.at[rd, lax.rem(z + d, 8)], g_r1.at[rd, d - 1], gram.at[0], z_dev(d))

        def cross_of(d):
            a = lax.rem(a_at + d, 8)
            term = jnp.dot(sk[...], act[:, columns(a * 256, 256)], preferred_element_type=F32)
            term = term.T.reshape(2, 8, 16, K)
            part[d - 1] = term
            s1[rd, d - 1] = term.astype(BF16)

        def cross_to(d):
            cross_of(d)
            send(s1.at[rd, d - 1, 0], r1a.at[rd, d - 1], cross.at[1], a_dev(d))

        def along_b(half):
            each(1, 8, lambda d: send(
                s1.at[rd, pl.ds(4 * half, 4), 1, lax.rem(b_at + d, 8)],
                r1b.at[rd, half, d - 1], cross.at[2 * half], b_dev(d)))

        each(1, 5, cross_to)
        arrived(g_r1.at[rd], gram.at[0])
        total = g_loc[rd, z]
        for d in range(7):
            total = total + g_r1[rd, d]
        g_r2[rd, y] = total
        for d in FAR:
            send(g_r2.at[rd, y], g_r2.at[rd, y], gram.at[1], y_dev(d))
        each(5, 7, cross_to)
        arrived(g_r2.at[rd, pl.ds(0, 7)], gram.at[1])
        total = g_r2[rd, 0]
        for d in range(1, 8):
            total = total + g_r2[rd, d]
        g_r3[rd, x] = total
        for d in (2, 1, 3):
            send(g_r3.at[rd, x], g_r3.at[rd, x], gram.at[2], x_dev(d))
        along_b(0)
        each(7, 8, cross_to)
        cross_of(8)
        along_b(1)
        arrived(g_r3.at[rd, pl.ds(0, 3)], gram.at[2])
        total = g_r3[rd, 0]
        for d in range(1, 4):
            total = total + g_r3[rd, d]
        g_full[rd, z] = total
        for d in FAR:
            send(g_full.at[rd, z], g_full.at[rd, z], gram.at[3], z_dev(d))

        arrived(r1a.at[rd], cross.at[1])
        total_0 = part[7, 0]
        for d in range(7):
            total_0 = total_0 + r1a[rd, d].astype(F32)
        t0[rd] = total_0
        each(1, 8, lambda d: send(
            t0.at[rd, lax.rem(b_at + d, 8)], r2.at[rd, 0, d - 1], cross.at[3], b_dev(d)))
        for half in range(2):
            arrived(r1b.at[rd, half], cross.at[2 * half])
            total_1 = part[4 * half : 4 * half + 4, 1, b_at]
            for d in range(7):
                total_1 = total_1 + r1b[rd, half, d].astype(F32)
            t1[rd, 4 * half : 4 * half + 4] = total_1
        each(1, 8, lambda d: send(
            t1.at[rd, d - 1], r2.at[rd, 1, d - 1], cross.at[4], a_dev(d)))
        arrived(g_full.at[rd, pl.ds(0, 7)], gram.at[3])
        elim_g[...] = g_full[rd].reshape(K, K)
        elim_x[...] = (
            lax.broadcasted_iota(jnp.int32, (K, K), 0) == lax.broadcasted_iota(jnp.int32, (K, K), 1)
        ).astype(F32)
        eliminate(0)
        eliminate(4)
        arrived(r2.at[rd, 0], cross.at[3])
        arrived(r2.at[rd, 1], cross.at[4])
        sum_0, sum_1 = t0[rd, b_at], t1[rd, 7]
        for d in range(7):
            sum_0 = sum_0 + r2[rd, 0, d]
            sum_1 = sum_1 + r2[rd, 1, d]
        r3[rd, x, 0] = sum_0
        r3[rd, x, 1] = sum_1
        for d in (2, 1, 3):
            send(r3.at[rd, x], r3.at[rd, x], cross.at[5], x_dev(d))
        eliminate(8)
        arrived(r3.at[rd, pl.ds(0, NX - 1)], cross.at[5])
        whole = r3[rd, 0]
        for d in range(1, NX):
            whole = whole + r3[rd, d]
        return whole

    def finish(wide):
        return lax.dot_general(
            wide[...].reshape(256, K), linv[...], NT, precision=lax.Precision.HIGHEST,
            preferred_element_type=F32,
        ).reshape(2, 8, 16, K)

    whole = solve_round(0, y, z, y_dev, z_dev)
    wide = gathered.at[0]
    wide[0, z] = whole[0]
    wide[1, y] = whole[1]
    for d in FAR:
        send(wide.at[0, z], wide.at[0, z], gather_sem.at[0], z_dev(d))
        send(wide.at[1, y], wide.at[1, y], gather_sem.at[1], y_dev(d))
    eliminate(12)
    arrived(wide.at[0, pl.ds(0, 7)], gather_sem.at[0])
    arrived(wide.at[1, pl.ds(0, 7)], gather_sem.at[1])
    solved[...] = finish(wide)
    bt[y, 0] = solved[0].astype(BF16)
    bt[:, 1, z] = solved[1].astype(BF16)
    for d in FAR:
        send(bt.at[y, 0], bt.at[y, 0], gather_sem.at[2], y_dev(d))
        send(bt.at[:, 1, z], bt.at[:, 1, z], gather_sem.at[3], z_dev(d))
    first[c, 0] = solved[0, z]
    first[c, 1] = solved[1, y]
    send(first.at[c], first.at[c], gather_sem.at[4], sib)
    arrived(bt.at[pl.ds(0, 7), 0], gather_sem.at[2])
    arrived(bt.at[:, 0, pl.ds(0, 7)], gather_sem.at[3])
    both_halves(1, lambda rows: jnp.dot(
        rows, bt[...].reshape(2048, K), preferred_element_type=F32))

    wide = gathered.at[1]
    wide[:, y] = solve_round(1, z, y, z_dev, y_dev)
    for d in FAR:
        send(wide.at[:, y], wide.at[:, y], gather_sem.at[5], y_dev(d))
    eliminate(12)
    arrived(first.at[0], gather_sem.at[4])
    out_first[...] = first[lax.div(x, 2), lax.rem(x, 2), pl.ds(pl.multiple_of(8 * c, 8), 8), :]
    arrived(wide.at[:, pl.ds(0, 7)], gather_sem.at[5])
    out_second[...] = finish(wide).reshape(256, K)
    for ref, sems in sent:
        pltpu.make_async_copy(ref, ref, sems.at[0]).wait()


def on_device(activations, probe_matrix):
    vmem = pltpu.VMEM
    first_t, second_t = pl.pallas_call(
        kernel,
        out_shape=(
            jax.ShapeDtypeStruct((8, K), F32),
            jax.ShapeDtypeStruct((256, K), F32),
        ),
        in_specs=[pl.BlockSpec(memory_space=pltpu.HBM)] * 2,
        out_specs=(
            pl.BlockSpec(memory_space=pltpu.VMEM),
            pl.BlockSpec(memory_space=pltpu.VMEM),
        ),
        scratch_shapes=[
            vmem((2 * TOK, D // 2), BF16),
            vmem((K, 256), BF16),
            vmem((2, 4, 32, K), BF16),
            vmem((8, 2, 32, K), BF16),
            vmem((8, 2, 4, 32, K), BF16),
            vmem((2, 2, TOK, K), F32),
            vmem((2, 2, TOK, K), F32),
            vmem((K, 2 * TOK), BF16),
            vmem((2, 8, 16, K), F32),
            vmem((2, 7, 16, K), F32),
            vmem((2, 8, 16, K), F32),
            vmem((2, 4, 16, K), F32),
            vmem((2, 8, 16, K), F32),
            vmem((K, K), F32),
            vmem((K, K), F32),
            vmem((K, K), F32),
            vmem((8, 2, 8, 16, K), F32),
            vmem((2, 8, 2, 8, 16, K), BF16),
            vmem((2, 7, 8, 16, K), BF16),
            vmem((2, 2, 7, 4, 16, K), BF16),
            vmem((2, 8, 16, K), F32),
            vmem((2, 8, 16, K), F32),
            vmem((2, 2, 7, 16, K), F32),
            vmem((2, NX, 2, 16, K), F32),
            vmem((8, 2, 8, 16, K), BF16),
            vmem((2, 2, 8, 16, K), F32),
            vmem((2, 8, 16, K), F32),
            vmem((2, 2, 16, K), F32),
            pltpu.SemaphoreType.DMA((2,)),
            pltpu.SemaphoreType.DMA((5, 2)),
            pltpu.SemaphoreType.DMA((2, 2, 2)),
            pltpu.SemaphoreType.DMA((2, 4, 2)),
            pltpu.SemaphoreType.DMA((2, 6, 2)),
            pltpu.SemaphoreType.DMA((6, 2)),
        ],
        compiler_params=pltpu.CompilerParams(
            collective_id=0, has_side_effects=True, vmem_limit_bytes=52 * 1024 * 1024
        ),
        name="range_finder",
    )(activations, probe_matrix)
    return first_t.T, second_t.T


def solution(mesh):
    return jax.shard_map(
        on_device,
        mesh=mesh,
        in_specs=(P(("grp", "row"), None), P(None, "row")),
        out_specs=(P(None, ("grp", "row")), P(None, "row")),
        check_vma=False,
    )
```

```python
import jax
import jax.numpy as jnp
from jax import lax
from jax.experimental import pallas as pl
from jax.experimental.pallas import tpu as pltpu
from jax.sharding import PartitionSpec as P

MESH = pl.DeviceIdType.MESH
NX, NY, NZ = 4, 8, 8
K = 128
TOK = 512
D = 4096
F32, BF16 = jnp.float32, jnp.bfloat16
NT = (((1,), (1,)), ((), ()))
FAR = (4, 3, 5, 2, 6, 1, 7)


def each(low, high, body):
    def step(i, carry):
        body(i)
        return carry

    lax.fori_loop(low, high, step, 0)


def kernel(
    act_hbm, probe_hbm, out_first, out_second,
    act, p_in, p_own, p_line, p_full, half_out, half_in, sk,
    g_loc, g_r1, g_r2, g_r3, g_full, elim_g, elim_x, linv,
    part_a, part_b, s1a, s1b, s2b, ra, rb, r1a, r1b, t0, t1, r2, r3,
    bt, gathered, solved, first,
    in_sem, probe_sem, half_sem, gram_sem, cross_sem, far_sem, gather_sem, line_sem,
):
    grp, row = lax.axis_index("grp"), lax.axis_index("row")
    y, x = lax.div(grp, NX), lax.rem(grp, NX)
    z, c = lax.div(row, 2), lax.rem(row, 2)

    def z_dev(d):
        return (grp, lax.rem(z + d, NZ) * 2 + c)

    def y_dev(d):
        return (lax.rem(y + d, NY) * NX + x, row)

    def x_dev(d):
        return (y * NX + lax.rem(x + d, NX), row)

    sib = (grp, row + 1 - 2 * c)

    def send(src, dst, sems, dev):
        pltpu.make_async_remote_copy(
            src_ref=src, dst_ref=dst, send_sem=sems.at[0], recv_sem=sems.at[1],
            device_id=dev, device_id_type=MESH,
        ).start()

    sent = []

    def arrived(ref, sems):
        pltpu.make_async_copy(ref, ref, sems.at[1]).wait()
        sent.append((ref, sems))

    def columns(at, width):
        return pl.ds(pl.multiple_of(at, width), width)

    mine = columns(c * TOK, TOK)
    load_probe = pltpu.make_async_copy(probe_hbm, p_in, in_sem.at[1])
    load_probe.start()

    def load(a):
        pltpu.make_async_copy(
            act_hbm.at[:, columns(a * 512 + c * 256, 256)], act.at[mine, columns(a * 256, 256)], in_sem.at[0]
        ).start()

    each(0, 8, load)

    barrier = pltpu.get_barrier_semaphore()

    def greet(dev):
        pl.semaphore_signal(barrier, inc=1, device_id=dev, device_id_type=MESH)

    for d in (4, 3, 5, 2, 6, 1, 7):
        greet(z_dev(d))
        greet(y_dev(d))
    for d in (2, 1, 3):
        greet(x_dev(d))
    greet(sib)
    load_probe.wait()
    p_own[...] = p_in[...].T.reshape(2, 4, 32, K)
    y_part = lax.rem(y, 4)
    p_line[z, 0] = p_own[0, y_part]
    p_line[z, 1] = p_own[1, x]
    pl.semaphore_wait(barrier, 18)

    for d in (4, 3, 5, 2, 6, 1, 7):
        send(p_line.at[z], p_line.at[z], probe_sem.at[0], z_dev(d))

    def push(a):
        send(
            act_hbm.at[:, columns(a * 512 + (1 - c) * 256, 256)],
            act.at[mine, columns(a * 256, 256)], probe_sem.at[2], sib)

    each(0, 8, push)
    arrived(p_line.at[pl.ds(0, 7)], probe_sem.at[0])
    for d in (1, 7, 2 + 4 * c):
        send(p_line.at[:, 0], p_full.at[:, 0, y_part], probe_sem.at[3], y_dev(d))
    for d in (2, 1, 3):
        send(p_line.at[:, 1], p_full.at[:, 1, x], probe_sem.at[4], x_dev(d))
    p_full[:, 0, y_part] = p_line[:, 0]
    p_full[:, 1, x] = p_line[:, 1]
    own_half = act.at[pl.ds(0, TOK)]
    pltpu.make_async_copy(own_half, own_half, in_sem.at[0]).wait()
    arrived(own_half, probe_sem.at[2])
    arrived(p_full.at[:, 0, pl.ds(0, 3)], probe_sem.at[3])
    arrived(p_full.at[:, 0, pl.ds(0, 3)], probe_sem.at[4])

    def both_halves(rd, product):
        def partial(q):
            half_out[rd, q] = product(act[columns(q * TOK, TOK), :])
            send(half_out.at[rd, q], half_in.at[rd, q], half_sem.at[rd, q], sib)

        each(0, 2, partial)
        for q in range(2):
            arrived(half_in.at[rd, q], half_sem.at[rd, q])
            sk[:, q * TOK : q * TOK + TOK] = (half_out[rd, q] + half_in[rd, q]).T.astype(BF16)

    both_halves(0, lambda rows: jnp.dot(
        rows, p_full[...].reshape(2048, K), preferred_element_type=F32))

    sublane = lax.broadcasted_iota(jnp.int32, (8, K), 0)

    def spread(line):
        return jnp.broadcast_to(line, (8, K))

    def block_step(left, right, at):
        rows, lane = left.shape[0], at * 8
        pivot = [spread(left[0:8, lane + j : lane + j + 1]) for j in range(8)]
        d = [[spread(pivot[j][i : i + 1, :]) if i >= j else None for j in range(8)] for i in range(8)]
        g = [spread(left[j : j + 1, :]) for j in range(8)]
        x = [spread(right[j : j + 1, :]) for j in range(8)]
        scale = []
        for k in range(8):
            scale.append(lax.rsqrt(d[k][k]))
            for i in range(k + 1, 8):
                d[i][k] = d[i][k] * scale[k]
            for j in range(k + 1, 8):
                for i in range(j, 8):
                    d[i][j] = d[i][j] - d[i][k] * d[j][k]
            g[k] = g[k] * scale[k]
            x[k] = x[k] * scale[k]
            for j in range(k + 1, 8):
                g[j] = g[j] - d[j][k] * g[k]
                x[j] = x[j] - d[j][k] * x[k]
        done = x[0]
        for k in range(1, 8):
            done = jnp.where(sublane == k, x[k], done)
        linv[at * 8 : at * 8 + 8, :] = done
        if rows == 8:
            return None, None
        for k in range(7, -1, -1):
            g[k] = g[k] * scale[k]
            x[k] = x[k] * scale[k]
            for j in range(k):
                g[j] = g[j] - d[k][j] * g[k]
                x[j] = x[j] - d[k][j] * x[k]
        groups = (rows - 8) // 8
        rest, right = left[8:, :].reshape(groups, 8, K), right[8:, :].reshape(groups, 8, K)
        below = rest
        for k in range(8):
            col = jnp.broadcast_to(below[:, :, lane + k : lane + k + 1], (groups, 8, K))
            rest = rest - col * g[k][None]
            right = right - col * x[k][None]
        return rest.reshape(rows - 8, K), right.reshape(rows - 8, K)

    def eliminate(start):
        rows = K - 8 * start
        left, right = elim_g[0:rows, :], elim_x[0:rows, :]
        for at in range(start, start + 4):
            left, right = block_step(left, right, at)
        if left is not None:
            elim_g[0 : rows - 32, :] = left
            elim_x[0 : rows - 32, :] = right

    def solve_round(rd, a_at, b_at, a_dev, b_dev):
        gram = gram_sem.at[rd]
        cross = cross_sem.at[rd]
        sketch = sk[...]
        g_loc[rd] = lax.dot_general(sketch, sketch, NT, preferred_element_type=F32).reshape(8, 16, K)
        for d in FAR:
            send(g_loc.at[rd, lax.rem(z + d, 8)], g_r1.at[rd, d - 1], gram.at[0], z_dev(d))

        turn = 2 + 4 * c

        def cross_of(d, at):
            a = lax.rem(a_at + d, 8)
            term = jnp.dot(sk[...], act[:, columns(a * 256, 256)], preferred_element_type=F32)
            term = term.T.reshape(2, 8, 16, K)
            part_b[at] = term[1]
            s1b[rd, at] = term[1].astype(BF16)
            return term[0]

        def far(k):
            slot = lax.rem(k + 2, 3)
            s1a[rd, k] = cross_of(4 - k + 3 * lax.div(k, 2), k).astype(BF16)
            send(s1a.at[rd, k], ra.at[rd, slot], cross.at[6], a_dev(jnp.where(k == 0, turn, 6 * k - 5)))

        def near(k):
            s1a[rd, 3 + k] = cross_of(1 + 6 * k, 3 + k).astype(BF16)
            send(s1a.at[rd, 3 + k], r1a.at[rd, k], cross.at[1], a_dev(1 + 6 * k))

        def middle(k):
            term = cross_of(2 + 4 * k, 5 + k)
            shared = ra[rd, 2].astype(F32) * (k == c).astype(F32)
            s1a[rd, 5 + k] = (term + ra[rd, k].astype(F32) + shared).astype(BF16)
            send(s1a.at[rd, 5 + k], r1a.at[rd, 2 + k], cross.at[1], a_dev(2 + 4 * k))

        def b_block(half, e):
            return s1b.at[rd, pl.ds(4 * half, 4), lax.rem(b_at + e, 8)]

        def start_b(half):
            send(b_block(half, 4), rb.at[rd, half, 2], far_sem.at[rd, half], b_dev(turn))
            send(b_block(half, 3), rb.at[rd, half, 0], far_sem.at[rd, half], b_dev(1))
            send(b_block(half, 5), rb.at[rd, half, 1], far_sem.at[rd, half], b_dev(7))
            for k in range(2):
                send(b_block(half, 1 + 6 * k), r1b.at[rd, half, k], cross.at[2 * half], b_dev(1 + 6 * k))

        def end_b(half):
            arrived(rb.at[rd, half], far_sem.at[rd, half])
            for k in range(2):
                term = part_b[4 * half : 4 * half + 4, lax.rem(b_at + 2 + 4 * k, 8)]
                shared = rb[rd, half, 2].astype(F32) * (k == c).astype(F32)
                s2b[rd, half, k] = (term + rb[rd, half, k].astype(F32) + shared).astype(BF16)
                send(s2b.at[rd, half, k], r1b.at[rd, half, 2 + k], cross.at[2 * half], b_dev(2 + 4 * k))

        each(0, 3, far)
        each(0, 2, near)
        arrived(g_r1.at[rd], gram.at[0])
        total = g_loc[rd, z]
        for d in range(7):
            total = total + g_r1[rd, d]
        g_r2[rd, y] = total
        for d in FAR:
            send(g_r2.at[rd, y], g_r2.at[rd, y], gram.at[1], y_dev(d))
        start_b(0)
        arrived(ra.at[rd], cross.at[6])
        each(0, 2, middle)
        arrived(g_r2.at[rd, pl.ds(0, 7)], gram.at[1])
        total = g_r2[rd, 0]
        for d in range(1, 8):
            total = total + g_r2[rd, d]
        g_r3[rd, x] = total
        for d in (2, 1, 3):
            send(g_r3.at[rd, x], g_r3.at[rd, x], gram.at[2], x_dev(d))
        part_a[...] = cross_of(0, 7)
        start_b(1)
        end_b(0)
        arrived(g_r3.at[rd, pl.ds(0, 3)], gram.at[2])
        total = g_r3[rd, 0]
        for d in range(1, 4):
            total = total + g_r3[rd, d]
        g_full[rd, z] = total
        for d in FAR:
            send(g_full.at[rd, z], g_full.at[rd, z], gram.at[3], z_dev(d))
        end_b(1)

        arrived(r1a.at[rd], cross.at[1])
        total_0 = part_a[...]
        for d in range(4):
            total_0 = total_0 + r1a[rd, d].astype(F32)
        t0[rd] = total_0
        each(1, 8, lambda d: send(
            t0.at[rd, lax.rem(b_at + d, 8)], r2.at[rd, 0, d - 1], cross.at[3], b_dev(d)))
        arrived(g_full.at[rd, pl.ds(0, 7)], gram.at[3])
        elim_g[...] = g_full[rd].reshape(K, K)
        elim_x[...] = (
            lax.broadcasted_iota(jnp.int32, (K, K), 0) == lax.broadcasted_iota(jnp.int32, (K, K), 1)
        ).astype(F32)
        eliminate(0)
        for half in range(2):
            arrived(r1b.at[rd, half], cross.at[2 * half])
            total_1 = part_b[4 * half : 4 * half + 4, b_at]
            for d in range(4):
                total_1 = total_1 + r1b[rd, half, d].astype(F32)
            t1[rd, 4 * half : 4 * half + 4] = total_1
        for at, d in enumerate((4, 3, 5, 1, 7, 2, 6)):
            send(t1.at[rd, at], r2.at[rd, 1, at], cross.at[4], a_dev(d))
        eliminate(4)
        arrived(r2.at[rd, 0], cross.at[3])
        arrived(r2.at[rd, 1], cross.at[4])
        sum_0, sum_1 = t0[rd, b_at], t1[rd, 7]
        for d in range(7):
            sum_0 = sum_0 + r2[rd, 0, d]
            sum_1 = sum_1 + r2[rd, 1, d]
        r3[rd, x, 0] = sum_0
        r3[rd, x, 1] = sum_1
        for d in (2, 1, 3):
            send(r3.at[rd, x], r3.at[rd, x], cross.at[5], x_dev(d))
        eliminate(8)
        arrived(r3.at[rd, pl.ds(0, NX - 1)], cross.at[5])
        whole = r3[rd, 0]
        for d in range(1, NX):
            whole = whole + r3[rd, d]
        return whole

    def finish(wide):
        return lax.dot_general(
            wide[...].reshape(256, K), linv[...], NT, precision=lax.Precision.HIGHEST,
            preferred_element_type=F32,
        ).reshape(2, 8, 16, K)

    whole = solve_round(0, y, z, y_dev, z_dev)
    wide = gathered.at[0]
    wide[0, z] = whole[0]
    wide[1, y] = whole[1]
    for d in FAR:
        send(wide.at[0, z], wide.at[0, z], gather_sem.at[0], z_dev(d))
        send(wide.at[1, y], wide.at[1, y], gather_sem.at[1], y_dev(d))
    eliminate(12)
    arrived(wide.at[0, pl.ds(0, 7)], gather_sem.at[0])
    arrived(wide.at[1, pl.ds(0, 7)], gather_sem.at[1])
    solved[...] = finish(wide)
    bt[y, 0] = solved[0].astype(BF16)
    bt[:, 1, z] = solved[1].astype(BF16)
    def of_y(d):
        return bt.at[lax.rem(y + d, 8), 0]

    def of_z(d):
        return bt.at[:, 1, lax.rem(z + d, 8)]

    axes = ((of_y, y_dev, line_sem.at[0]), (of_z, z_dev, line_sem.at[1]))
    for k, d in ((1, 2), (2, 6), (0, 1), (0, 7)):
        for block, dev, sems in axes:
            send(block(0), block(0), sems.at[k], dev(d))
    first[c, 0] = solved[0, z]
    first[c, 1] = solved[1, y]
    send(first.at[c], first.at[c], gather_sem.at[4], sib)
    piece = bt.at[0, 0]
    for k, d in ((1, 6), (2, 2)):
        for block, dev, sems in axes:
            arrived(piece, sems.at[k])
            send(block(d), block(d), sems.at[3], dev(1 if d == 6 else 7))
    turned = 6 - 4 * c
    for block, dev, sems in axes:
        send(block(turned), block(turned), sems.at[3], dev(2 + 4 * c))
    for block, dev, sems in axes:
        arrived(bt.at[pl.ds(0, 2), 0], sems.at[0])
        arrived(bt.at[pl.ds(0, 3), 0], sems.at[3])
    both_halves(1, lambda rows: jnp.dot(
        rows, bt[...].reshape(2048, K), preferred_element_type=F32))

    wide = gathered.at[1]
    wide[:, y] = solve_round(1, z, y, z_dev, y_dev)
    for d in FAR:
        send(wide.at[:, y], wide.at[:, y], gather_sem.at[5], y_dev(d))
    eliminate(12)
    arrived(first.at[0], gather_sem.at[4])
    out_first[...] = first[lax.div(x, 2), lax.rem(x, 2), pl.ds(pl.multiple_of(8 * c, 8), 8), :]
    arrived(wide.at[:, pl.ds(0, 7)], gather_sem.at[5])
    out_second[...] = finish(wide).reshape(256, K)
    for ref, sems in sent:
        pltpu.make_async_copy(ref, ref, sems.at[0]).wait()


def on_device(activations, probe_matrix):
    vmem = pltpu.VMEM
    first_t, second_t = pl.pallas_call(
        kernel,
        out_shape=(
            jax.ShapeDtypeStruct((8, K), F32),
            jax.ShapeDtypeStruct((256, K), F32),
        ),
        in_specs=[pl.BlockSpec(memory_space=pltpu.HBM)] * 2,
        out_specs=(
            pl.BlockSpec(memory_space=pltpu.VMEM),
            pl.BlockSpec(memory_space=pltpu.VMEM),
        ),
        scratch_shapes=[
            vmem((2 * TOK, D // 2), BF16),
            vmem((K, 256), BF16),
            vmem((2, 4, 32, K), BF16),
            vmem((8, 2, 32, K), BF16),
            vmem((8, 2, 4, 32, K), BF16),
            vmem((2, 2, TOK, K), F32),
            vmem((2, 2, TOK, K), F32),
            vmem((K, 2 * TOK), BF16),
            vmem((2, 8, 16, K), F32),
            vmem((2, 7, 16, K), F32),
            vmem((2, 8, 16, K), F32),
            vmem((2, 4, 16, K), F32),
            vmem((2, 8, 16, K), F32),
            vmem((K, K), F32),
            vmem((K, K), F32),
            vmem((K, K), F32),
            vmem((8, 16, K), F32),
            vmem((8, 8, 16, K), F32),
            vmem((2, 7, 8, 16, K), BF16),
            vmem((2, 8, 8, 16, K), BF16),
            vmem((2, 2, 2, 4, 16, K), BF16),
            vmem((2, 3, 8, 16, K), BF16),
            vmem((2, 2, 3, 4, 16, K), BF16),
            vmem((2, 4, 8, 16, K), BF16),
            vmem((2, 2, 4, 4, 16, K), BF16),
            vmem((2, 8, 16, K), F32),
            vmem((2, 8, 16, K), F32),
            vmem((2, 2, 7, 16, K), F32),
            vmem((2, NX, 2, 16, K), F32),
            vmem((8, 2, 8, 16, K), BF16),
            vmem((2, 2, 8, 16, K), F32),
            vmem((2, 8, 16, K), F32),
            vmem((2, 2, 16, K), F32),
            pltpu.SemaphoreType.DMA((2,)),
            pltpu.SemaphoreType.DMA((5, 2)),
            pltpu.SemaphoreType.DMA((2, 2, 2)),
            pltpu.SemaphoreType.DMA((2, 4, 2)),
            pltpu.SemaphoreType.DMA((2, 7, 2)),
            pltpu.SemaphoreType.DMA((2, 2, 2)),
            pltpu.SemaphoreType.DMA((6, 2)),
            pltpu.SemaphoreType.DMA((2, 4, 2)),
        ],
        compiler_params=pltpu.CompilerParams(
            collective_id=0, has_side_effects=True, vmem_limit_bytes=52 * 1024 * 1024
        ),
        name="range_finder",
    )(activations, probe_matrix)
    return first_t.T, second_t.T


def solution(mesh):
    return jax.shard_map(
        on_device,
        mesh=mesh,
        in_specs=(P(("grp", "row"), None), P(None, "row")),
        out_specs=(P(None, ("grp", "row")), P(None, "row")),
        check_vma=False,
    )
```

```python
import jax
import jax.numpy as jnp
from jax import lax
from jax.experimental import pallas as pl
from jax.experimental.pallas import tpu as pltpu
from jax.sharding import PartitionSpec as P

MESH = pl.DeviceIdType.MESH
NX, NY, NZ = 4, 8, 8
K = 128
TOK = 512
D = 4096
F32, BF16 = jnp.float32, jnp.bfloat16
NT = (((1,), (1,)), ((), ()))
FAR = (4, 3, 5, 2, 6, 1, 7)


def each(low, high, body):
    def step(i, carry):
        body(i)
        return carry

    lax.fori_loop(low, high, step, 0)


def kernel(
    act_hbm, probe_hbm, out_first, out_second,
    act, p_in, p_own, p_line, p_full, half_out, half_in, sk,
    g_loc, g_r1, g_r2, g_r3, g_full, elim_g, elim_x, linv,
    part, s1, r1a, r1b, t0, t1, r2, r3,
    bt, gathered, solved, first,
    in_sem, probe_sem, half_sem, gram_sem, cross_sem, gather_sem,
):
    grp, row = lax.axis_index("grp"), lax.axis_index("row")
    y, x = lax.div(grp, NX), lax.rem(grp, NX)
    z, c = lax.div(row, 2), lax.rem(row, 2)

    def z_dev(d):
        return (grp, lax.rem(z + d, NZ) * 2 + c)

    def y_dev(d):
        return (lax.rem(y + d, NY) * NX + x, row)

    def x_dev(d):
        return (y * NX + lax.rem(x + d, NX), row)

    sib = (grp, row + 1 - 2 * c)

    def send(src, dst, sems, dev):
        pltpu.make_async_remote_copy(
            src_ref=src, dst_ref=dst, send_sem=sems.at[0], recv_sem=sems.at[1],
            device_id=dev, device_id_type=MESH,
        ).start()

    sent = []

    def arrived(ref, sems):
        pltpu.make_async_copy(ref, ref, sems.at[1]).wait()
        sent.append((ref, sems))

    def columns(at, width):
        return pl.ds(pl.multiple_of(at, width), width)

    mine = columns(c * TOK, TOK)
    load_probe = pltpu.make_async_copy(probe_hbm, p_in, in_sem.at[1])
    load_probe.start()

    def load(a):
        pltpu.make_async_copy(
            act_hbm.at[:, columns(a * 512 + c * 256, 256)], act.at[mine, columns(a * 256, 256)], in_sem.at[0]
        ).start()

    each(0, 8, load)

    barrier = pltpu.get_barrier_semaphore()

    def greet(dev):
        pl.semaphore_signal(barrier, inc=1, device_id=dev, device_id_type=MESH)

    for d in (4, 3, 5, 2, 6, 1, 7):
        greet(z_dev(d))
        greet(y_dev(d))
    for d in (2, 1, 3):
        greet(x_dev(d))
    greet(sib)
    load_probe.wait()
    p_own[...] = p_in[...].T.reshape(2, 4, 32, K)
    y_part = lax.rem(y, 4)
    p_line[z, 0] = p_own[0, y_part]
    p_line[z, 1] = p_own[1, x]
    pl.semaphore_wait(barrier, 18)

    for d in (4, 3, 5, 2, 6, 1, 7):
        send(p_line.at[z], p_line.at[z], probe_sem.at[0], z_dev(d))

    def push(a):
        send(
            act_hbm.at[:, columns(a * 512 + (1 - c) * 256, 256)],
            act.at[mine, columns(a * 256, 256)], probe_sem.at[2], sib)

    each(0, 8, push)
    arrived(p_line.at[pl.ds(0, 7)], probe_sem.at[0])
    for d in (1, 7, 2 + 4 * c):
        send(p_line.at[:, 0], p_full.at[:, 0, y_part], probe_sem.at[3], y_dev(d))
    for d in (2, 1, 3):
        send(p_line.at[:, 1], p_full.at[:, 1, x], probe_sem.at[4], x_dev(d))
    p_full[:, 0, y_part] = p_line[:, 0]
    p_full[:, 1, x] = p_line[:, 1]
    own_half = act.at[pl.ds(0, TOK)]
    pltpu.make_async_copy(own_half, own_half, in_sem.at[0]).wait()
    arrived(own_half, probe_sem.at[2])
    arrived(p_full.at[:, 0, pl.ds(0, 3)], probe_sem.at[3])
    arrived(p_full.at[:, 0, pl.ds(0, 3)], probe_sem.at[4])

    def both_halves(rd, product):
        def partial(q):
            half_out[rd, q] = product(act[columns(q * TOK, TOK), :])
            send(half_out.at[rd, q], half_in.at[rd, q], half_sem.at[rd, q], sib)

        each(0, 2, partial)
        for q in range(2):
            arrived(half_in.at[rd, q], half_sem.at[rd, q])
            sk[:, q * TOK : q * TOK + TOK] = (half_out[rd, q] + half_in[rd, q]).T.astype(BF16)

    both_halves(0, lambda rows: jnp.dot(
        rows, p_full[...].reshape(2048, K), preferred_element_type=F32))

    sublane = lax.broadcasted_iota(jnp.int32, (8, K), 0)

    def spread(line):
        return jnp.broadcast_to(line, (8, K))

    def block_step(left, right, at):
        rows, lane = left.shape[0], at * 8
        pivot = [spread(left[0:8, lane + j : lane + j + 1]) for j in range(8)]
        d = [[spread(pivot[j][i : i + 1, :]) if i >= j else None for j in range(8)] for i in range(8)]
        g = [spread(left[j : j + 1, :]) for j in range(8)]
        x = [spread(right[j : j + 1, :]) for j in range(8)]
        scale = []
        for k in range(8):
            scale.append(lax.rsqrt(d[k][k]))
            for i in range(k + 1, 8):
                d[i][k] = d[i][k] * scale[k]
            for j in range(k + 1, 8):
                for i in range(j, 8):
                    d[i][j] = d[i][j] - d[i][k] * d[j][k]
            g[k] = g[k] * scale[k]
            x[k] = x[k] * scale[k]
            for j in range(k + 1, 8):
                g[j] = g[j] - d[j][k] * g[k]
                x[j] = x[j] - d[j][k] * x[k]
        done = x[0]
        for k in range(1, 8):
            done = jnp.where(sublane == k, x[k], done)
        linv[at * 8 : at * 8 + 8, :] = done
        if rows == 8:
            return None, None
        for k in range(7, -1, -1):
            g[k] = g[k] * scale[k]
            x[k] = x[k] * scale[k]
            for j in range(k):
                g[j] = g[j] - d[k][j] * g[k]
                x[j] = x[j] - d[k][j] * x[k]
        groups = (rows - 8) // 8
        rest, right = left[8:, :].reshape(groups, 8, K), right[8:, :].reshape(groups, 8, K)
        below = rest
        for k in range(8):
            col = jnp.broadcast_to(below[:, :, lane + k : lane + k + 1], (groups, 8, K))
            rest = rest - col * g[k][None]
            right = right - col * x[k][None]
        return rest.reshape(rows - 8, K), right.reshape(rows - 8, K)

    def eliminate(start):
        rows = K - 8 * start
        left, right = elim_g[0:rows, :], elim_x[0:rows, :]
        for at in range(start, start + 4):
            left, right = block_step(left, right, at)
        if left is not None:
            elim_g[0 : rows - 32, :] = left
            elim_x[0 : rows - 32, :] = right

    def solve_round(rd, a_at, b_at, a_dev, b_dev):
        gram = gram_sem.at[rd]
        cross = cross_sem.at[rd]
        sketch = sk[...]
        g_loc[rd] = lax.dot_general(sketch, sketch, NT, preferred_element_type=F32).reshape(8, 16, K)
        for d in FAR:
            send(g_loc.at[rd, lax.rem(z + d, 8)], g_r1.at[rd, d - 1], gram.at[0], z_dev(d))

        def cross_of(d):
            a = lax.rem(a_at + d, 8)
            term = jnp.dot(sk[...], act[:, columns(a * 256, 256)], preferred_element_type=F32)
            term = term.T.reshape(2, 8, 16, K)
            part[d - 1] = term
            s1[rd, d - 1] = term.astype(BF16)

        def cross_to(d):
            cross_of(d)
            send(s1.at[rd, d - 1, 0], r1a.at[rd, d - 1], cross.at[1], a_dev(d))

        def along_b(half):
            each(1, 8, lambda d: send(
                s1.at[rd, pl.ds(4 * half, 4), 1, lax.rem(b_at + d, 8)],
                r1b.at[rd, half, d - 1], cross.at[2 * half], b_dev(d)))

        each(1, 5, cross_to)
        arrived(g_r1.at[rd], gram.at[0])
        total = g_loc[rd, z]
        for d in range(7):
            total = total + g_r1[rd, d]
        g_r2[rd, y] = total
        for d in FAR:
            send(g_r2.at[rd, y], g_r2.at[rd, y], gram.at[1], y_dev(d))
        along_b(0)
        each(5, 8, cross_to)
        arrived(g_r2.at[rd, pl.ds(0, 7)], gram.at[1])
        total = g_r2[rd, 0]
        for d in range(1, 8):
            total = total + g_r2[rd, d]
        g_r3[rd, x] = total
        for d in (2, 1, 3):
            send(g_r3.at[rd, x], g_r3.at[rd, x], gram.at[2], x_dev(d))
        cross_of(8)
        along_b(1)
        arrived(g_r3.at[rd, pl.ds(0, 3)], gram.at[2])
        total = g_r3[rd, 0]
        for d in range(1, 4):
            total = total + g_r3[rd, d]
        g_full[rd, z] = total
        for d in FAR:
            send(g_full.at[rd, z], g_full.at[rd, z], gram.at[3], z_dev(d))

        arrived(r1a.at[rd], cross.at[1])
        total_0 = part[7, 0]
        for d in range(7):
            total_0 = total_0 + r1a[rd, d].astype(F32)
        t0[rd] = total_0
        each(1, 8, lambda d: send(
            t0.at[rd, lax.rem(b_at + d, 8)], r2.at[rd, 0, d - 1], cross.at[3], b_dev(d)))
        arrived(g_full.at[rd, pl.ds(0, 7)], gram.at[3])
        elim_g[...] = g_full[rd].reshape(K, K)
        elim_x[...] = (
            lax.broadcasted_iota(jnp.int32, (K, K), 0) == lax.broadcasted_iota(jnp.int32, (K, K), 1)
        ).astype(F32)
        eliminate(0)
        for half in range(2):
            arrived(r1b.at[rd, half], cross.at[2 * half])
            total_1 = part[4 * half : 4 * half + 4, 1, b_at]
            for d in range(7):
                total_1 = total_1 + r1b[rd, half, d].astype(F32)
            t1[rd, 4 * half : 4 * half + 4] = total_1
        each(1, 8, lambda d: send(
            t1.at[rd, d - 1], r2.at[rd, 1, d - 1], cross.at[4], a_dev(d)))
        eliminate(4)
        arrived(r2.at[rd, 0], cross.at[3])
        arrived(r2.at[rd, 1], cross.at[4])
        sum_0, sum_1 = t0[rd, b_at], t1[rd, 7]
        for d in range(7):
            sum_0 = sum_0 + r2[rd, 0, d]
            sum_1 = sum_1 + r2[rd, 1, d]
        r3[rd, x, 0] = sum_0
        r3[rd, x, 1] = sum_1
        for d in (2, 1, 3):
            send(r3.at[rd, x], r3.at[rd, x], cross.at[5], x_dev(d))
        eliminate(8)
        arrived(r3.at[rd, pl.ds(0, NX - 1)], cross.at[5])
        whole = r3[rd, 0]
        for d in range(1, NX):
            whole = whole + r3[rd, d]
        return whole

    def finish(wide):
        return lax.dot_general(
            wide[...].reshape(256, K), linv[...], NT, precision=lax.Precision.HIGHEST,
            preferred_element_type=F32,
        ).reshape(2, 8, 16, K)

    whole = solve_round(0, y, z, y_dev, z_dev)
    wide = gathered.at[0]
    wide[0, z] = whole[0]
    wide[1, y] = whole[1]
    for d in FAR:
        send(wide.at[0, z], wide.at[0, z], gather_sem.at[0], z_dev(d))
        send(wide.at[1, y], wide.at[1, y], gather_sem.at[1], y_dev(d))
    eliminate(12)
    arrived(wide.at[0, pl.ds(0, 7)], gather_sem.at[0])
    arrived(wide.at[1, pl.ds(0, 7)], gather_sem.at[1])
    solved[...] = finish(wide)
    bt[y, 0] = solved[0].astype(BF16)
    bt[:, 1, z] = solved[1].astype(BF16)
    for d in FAR:
        send(bt.at[y, 0], bt.at[y, 0], gather_sem.at[2], y_dev(d))
        send(bt.at[:, 1, z], bt.at[:, 1, z], gather_sem.at[3], z_dev(d))
    first[c, 0] = solved[0, z]
    first[c, 1] = solved[1, y]
    send(first.at[c], first.at[c], gather_sem.at[4], sib)
    arrived(bt.at[pl.ds(0, 7), 0], gather_sem.at[2])
    arrived(bt.at[:, 0, pl.ds(0, 7)], gather_sem.at[3])
    both_halves(1, lambda rows: jnp.dot(
        rows, bt[...].reshape(2048, K), preferred_element_type=F32))

    wide = gathered.at[1]
    wide[:, y] = solve_round(1, z, y, z_dev, y_dev)
    for d in FAR:
        send(wide.at[:, y], wide.at[:, y], gather_sem.at[5], y_dev(d))
    eliminate(12)
    arrived(first.at[0], gather_sem.at[4])
    out_first[...] = first[lax.div(x, 2), lax.rem(x, 2), pl.ds(pl.multiple_of(8 * c, 8), 8), :]
    arrived(wide.at[:, pl.ds(0, 7)], gather_sem.at[5])
    out_second[...] = finish(wide).reshape(256, K)
    for ref, sems in sent:
        pltpu.make_async_copy(ref, ref, sems.at[0]).wait()


def on_device(activations, probe_matrix):
    vmem = pltpu.VMEM
    first_t, second_t = pl.pallas_call(
        kernel,
        out_shape=(
            jax.ShapeDtypeStruct((8, K), F32),
            jax.ShapeDtypeStruct((256, K), F32),
        ),
        in_specs=[pl.BlockSpec(memory_space=pltpu.HBM)] * 2,
        out_specs=(
            pl.BlockSpec(memory_space=pltpu.VMEM),
            pl.BlockSpec(memory_space=pltpu.VMEM),
        ),
        scratch_shapes=[
            vmem((2 * TOK, D // 2), BF16),
            vmem((K, 256), BF16),
            vmem((2, 4, 32, K), BF16),
            vmem((8, 2, 32, K), BF16),
            vmem((8, 2, 4, 32, K), BF16),
            vmem((2, 2, TOK, K), F32),
            vmem((2, 2, TOK, K), F32),
            vmem((K, 2 * TOK), BF16),
            vmem((2, 8, 16, K), F32),
            vmem((2, 7, 16, K), F32),
            vmem((2, 8, 16, K), F32),
            vmem((2, 4, 16, K), F32),
            vmem((2, 8, 16, K), F32),
            vmem((K, K), F32),
            vmem((K, K), F32),
            vmem((K, K), F32),
            vmem((8, 2, 8, 16, K), F32),
            vmem((2, 8, 2, 8, 16, K), BF16),
            vmem((2, 7, 8, 16, K), BF16),
            vmem((2, 2, 7, 4, 16, K), BF16),
            vmem((2, 8, 16, K), F32),
            vmem((2, 8, 16, K), F32),
            vmem((2, 2, 7, 16, K), F32),
            vmem((2, NX, 2, 16, K), F32),
            vmem((8, 2, 8, 16, K), BF16),
            vmem((2, 2, 8, 16, K), F32),
            vmem((2, 8, 16, K), F32),
            vmem((2, 2, 16, K), F32),
            pltpu.SemaphoreType.DMA((2,)),
            pltpu.SemaphoreType.DMA((5, 2)),
            pltpu.SemaphoreType.DMA((2, 2, 2)),
            pltpu.SemaphoreType.DMA((2, 4, 2)),
            pltpu.SemaphoreType.DMA((2, 6, 2)),
            pltpu.SemaphoreType.DMA((6, 2)),
        ],
        compiler_params=pltpu.CompilerParams(
            collective_id=0, has_side_effects=True, vmem_limit_bytes=52 * 1024 * 1024
        ),
        name="range_finder",
    )(activations, probe_matrix)
    return first_t.T, second_t.T


def solution(mesh):
    return jax.shard_map(
        on_device,
        mesh=mesh,
        in_specs=(P(("grp", "row"), None), P(None, "row")),
        out_specs=(P(None, ("grp", "row")), P(None, "row")),
        check_vma=False,
    )
```
